128 devices in a mesh: ta: 8 (over y_lo, z), gz: 4 (over x), xy: 4 (over y_hi, core).
Axes of the slice: x: 4, y: 4 (y_hi: 2, y_lo: 2; y = y_hi * 2 + y_lo), z: 4, core: 2. Of those that a mesh axis runs over, the one named last changes fastest.
Arguments:
- fine_solution: bfloat16 [2, 4, 12, 32, 16, 512], P(None, None, None, 'ta', 'gz', 'xy'), may hold values from -6 to 6
- links: bfloat16 [8, 2, 3, 3, 32, 16, 512], P(None, None, None, None, 'ta', 'gz', 'xy'), may hold values from -3.5 to 3.5
- clover: bfloat16 [2, 2, 6, 6, 32, 16, 512], P(None, None, None, None, 'ta', 'gz', 'xy'), may hold values from -1.796875 to 1.796875
- near_null: bfloat16 [12, 2, 12, 32, 16, 512], P(None, None, None, 'ta', 'gz', 'xy'), may hold values from -0.15625 to 0.15625
- coarse_links: float32 [9, 2, 24, 24, 8, 4, 32], P(None, None, None, None, 'ta', 'gz', 'xy'), may hold values from -0.15 to 0.15
- wall_time: int32 [4], replicated, may hold values from 0 to 31
- spin_index: int32 [4], replicated, may hold values from 0 to 3, each once
- wall_colour: float32 [2, 4, 3], replicated, may hold values from -18 to 18
Outputs:
- corrected: float32 [2, 4, 12, 32, 16, 512], P(None, None, None, 'ta', 'gz', 'xy')
The draws below stay inside these ranges and needn't reach their ends.
Inputs may be any that keep to these rules, and one draw needn't show every extreme that they name: `spin_index`: each right-hand side has its own spin.
All inputs are finite; a program needn't handle non-finite values.
Results may differ from the reference program's by a relative error of at most 0.0003.
Values may be sent and summed in bfloat16 or wider, within the bound.
No kernel may reach another device: no remote copies, remote signals or barrier semaphores. Data moves between devices by JAX's collectives and lax.ppermute only.
A program may use at most 192 MiB of HBM per device.

```python
import jax
import jax.numpy as jnp
from jax import lax

RHS = 4
NVEC = 12
BLOCK = 4
ITERS = 4
NY = 32
NT = 32
NZ = 16
NX = 16


def touch_ends(entries, stream_key, least, high):
    longest = entries.shape.index(max(entries.shape))
    spots = []
    for shift in (0, 1):
        where = [jax.random.randint(jax.random.fold_in(stream_key, axis), (), 0, length) for axis, length in enumerate(entries.shape)]
        where[longest] = (where[longest] + shift) % entries.shape[longest]
        spots.append(tuple(where))
    return entries.at[spots[0]].set(least).at[spots[1]].set(high)


def shard_levels(rng, extent, pieces, least, high):
    def one(dim, parts):
        draws = jax.random.uniform(jax.random.fold_in(jax.random.fold_in(rng, 6), dim), (parts,), jnp.float32, least / len(pieces), high / len(pieces))
        return jnp.repeat(jnp.exp(draws), extent[dim] // parts).reshape((-1,) + (1,) * (len(extent) - dim - 1))

    level = one(*pieces[0])
    for cut in pieces[1:]:
        level = level * one(*cut)
    return level


def centred(key, shape, spread, most, split=(), kind=jnp.bfloat16):
    loudness = shard_levels(key, shape, split, -0.22, 0.18) if split else 1.0
    entries = jax.random.normal(key, shape, jnp.float32) * spread * loudness
    return jnp.minimum(jnp.maximum(entries, -most), most).astype(kind)


def setup_inputs(seed: int = 0) -> dict:
    splits = jax.random.split(jax.random.key(seed), 9)
    return {
        "fine_solution": centred(splits[0], (2, RHS, 12, NT, NZ, NX * NY), 1.0, 6.0, ((3, 8), (4, 4), (5, 4))),
        "links": centred(splits[1], (8, 2, 3, 3, NT, NZ, NX * NY), 3 ** -0.5, 3.5, ((4, 8), (5, 4), (6, 4))),
        "clover": centred(splits[2], (2, 2, 6, 6, NT, NZ, NX * NY), 0.3, 1.796875, ((4, 8), (5, 4), (6, 4))),
        "near_null": centred(splits[3], (NVEC, 2, 12, NT, NZ, NX * NY), (6 * BLOCK ** 4) ** -0.5, 0.15625, ((3, 8), (4, 4), (5, 4))),
        "coarse_links": centred(splits[4], (9, 2, 2 * NVEC, 2 * NVEC, NT // BLOCK, NZ // BLOCK, (NX // BLOCK) * (NY // BLOCK)), 0.025, 0.15, ((4, 8), (5, 4), (6, 4)), jnp.float32),
        "wall_time": touch_ends(jax.random.randint(splits[5], (RHS,), 0, NT), jax.random.fold_in(splits[5], 1), 0, NT - 1).astype(jnp.int32),
        "spin_index": jax.random.permutation(splits[6], RHS).astype(jnp.int32),
        "wall_colour": centred(splits[7], (2, RHS, 3), 3.0, 18.0, (), jnp.float32),
    }


gammas = [
    [[0j, 0j, 1 + 0j, 0j], [0j, 0j, 0j, 1 + 0j], [1 + 0j, 0j, 0j, 0j], [0j, 1 + 0j, 0j, 0j]],
    [[0j, 0j, 1j, 0j], [0j, 0j, 0j, -1j], [-1j, 0j, 0j, 0j], [0j, 1j, 0j, 0j]],
    [[0j, 0j, 0j, 1j], [0j, 0j, 1j, 0j], [0j, -1j, 0j, 0j], [-1j, 0j, 0j, 0j]],
    [[0j, 0j, 0j, -1 + 0j], [0j, 0j, 1 + 0j, 0j], [0j, 1 + 0j, 0j, 0j], [-1 + 0j, 0j, 0j, 0j]],
]
mass_term = 4.1


def project(sign, direction, field):
    field_re, field_im = field
    out_re = []
    out_im = []
    for spin_out in range(4):
        total_re = field_re[:, spin_out]
        total_im = field_im[:, spin_out]
        for spin_in in range(4):
            entry = gammas[direction][spin_out][spin_in] * sign
            if entry.real != 0:
                total_re = total_re + entry.real * field_re[:, spin_in]
                total_im = total_im + entry.real * field_im[:, spin_in]
            if entry.imag != 0:
                total_re = total_re - entry.imag * field_im[:, spin_in]
                total_im = total_im + entry.imag * field_re[:, spin_in]
        out_re.append(total_re)
        out_im.append(total_im)
    return jnp.stack(out_re, axis=1), jnp.stack(out_im, axis=1)


def color_apply(link, field):
    link_re = link[0][None, None]
    link_im = link[1][None, None]
    field_re = field[0][:, :, None]
    field_im = field[1][:, :, None]
    return (jnp.sum(link_re * field_re - link_im * field_im, axis=3),
            jnp.sum(link_re * field_im + link_im * field_re, axis=3))


def link_pair(links, which):
    return links[which, 0].astype(jnp.float32), links[which, 1].astype(jnp.float32)


def clover_apply(clover_blocks, field):
    rows = field[0].shape[0]
    sites = field[0].shape[3:]
    flat_re = field[0].reshape((rows, 12) + sites)
    flat_im = field[1].reshape((rows, 12) + sites)
    parts_re = []
    parts_im = []
    for chirality in range(2):
        block_re = flat_re[:, 6 * chirality:6 * chirality + 6][:, None]
        block_im = flat_im[:, 6 * chirality:6 * chirality + 6][:, None]
        entry_re = clover_blocks[chirality, 0].astype(jnp.float32)[None]
        entry_im = clover_blocks[chirality, 1].astype(jnp.float32)[None]
        parts_re.append(jnp.sum(entry_re * block_re - entry_im * block_im, axis=2))
        parts_im.append(jnp.sum(entry_re * block_im + entry_im * block_re, axis=2))
    return (jnp.concatenate(parts_re, axis=1).reshape((rows, 4, 3) + sites),
            jnp.concatenate(parts_im, axis=1).reshape((rows, 4, 3) + sites))


def wilson(center, uppers, lowers, links, clover_blocks):
    extra = clover_apply(clover_blocks, center)
    total_re = mass_term * center[0] + extra[0]
    total_im = mass_term * center[1] + extra[1]
    for direction in range(4):
        ahead = color_apply(link_pair(links, 2 * direction), project(-1.0, direction, uppers[direction]))
        behind = color_apply(link_pair(links, 2 * direction + 1), project(1.0, direction, lowers[direction]))
        total_re = total_re - 0.5 * (ahead[0] + behind[0])
        total_im = total_im - 0.5 * (ahead[1] + behind[1])
    return total_re, total_im


def make_source(wall_time, spin_index, wall_colour, offset, site_shape):
    rows = wall_time.shape[0]
    times = offset + jnp.arange(site_shape[0], dtype=jnp.int32)
    time_mask = (times[None, :] == wall_time[:, None]).astype(jnp.float32)
    spin_mask = (jnp.arange(4, dtype=jnp.int32)[None, :] == spin_index[:, None]).astype(jnp.float32)
    weight = (spin_mask[:, :, None, None] * time_mask[:, None, None, :])[..., None, None, None]
    full = (rows, 4, 3) + tuple(site_shape)
    source_re = jnp.broadcast_to(weight * wall_colour[0][:, None, :, None, None, None, None], full)
    source_im = jnp.broadcast_to(weight * wall_colour[1][:, None, :, None, None, None, None], full)
    return source_re, source_im


def block_sum(values):
    lead = values.shape[:-4]
    ext_t, ext_z, ext_x, ext_y = values.shape[-4:]
    shaped = values.reshape(lead + (ext_t // BLOCK, BLOCK, ext_z // BLOCK, BLOCK, ext_x // BLOCK, BLOCK, ext_y // BLOCK, BLOCK))
    start = len(lead)
    return jnp.sum(shaped, axis=(start + 1, start + 3, start + 5, start + 7))


def restrict(near_vectors, residual):
    halves_re = []
    halves_im = []
    for chirality in range(2):
        total_re = None
        total_im = None
        for component in range(6):
            position = 6 * chirality + component
            near_re = near_vectors[:, 0, position].astype(jnp.float32)[:, None]
            near_im = near_vectors[:, 1, position].astype(jnp.float32)[:, None]
            res_re = residual[0][:, position][None]
            res_im = residual[1][:, position][None]
            term_re = near_re * res_re + near_im * res_im
            term_im = near_re * res_im - near_im * res_re
            total_re = term_re if total_re is None else total_re + term_re
            total_im = term_im if total_im is None else total_im + term_im
        halves_re.append(block_sum(total_re))
        halves_im.append(block_sum(total_im))
    coarse_re = jnp.swapaxes(jnp.concatenate(halves_re, axis=0), 0, 1)
    coarse_im = jnp.swapaxes(jnp.concatenate(halves_im, axis=0), 0, 1)
    return jnp.stack((coarse_re, coarse_im))


def coarse_apply(estimate, uppers, lowers, stencil):
    def multiply(which, vector):
        entry_re = stencil[which, 0][None]
        entry_im = stencil[which, 1][None]
        vector_re = vector[0][:, None]
        vector_im = vector[1][:, None]
        return jnp.stack((jnp.sum(entry_re * vector_re - entry_im * vector_im, axis=2),
                          jnp.sum(entry_re * vector_im + entry_im * vector_re, axis=2)))

    total = multiply(0, estimate)
    for direction in range(4):
        total = total + multiply(1 + 2 * direction, uppers[direction]) + multiply(2 + 2 * direction, lowers[direction])
    return total


def prolong(near_vectors, coarse, site_shape):
    count = near_vectors.shape[0]
    rows = coarse.shape[1]
    agg_t, agg_z, agg_x, agg_y = coarse.shape[3:]
    shaped = coarse.reshape((2, rows, 2, count, agg_t, 1, agg_z, 1, agg_x, 1, agg_y, 1))
    shaped = jnp.broadcast_to(shaped, (2, rows, 2, count, agg_t, BLOCK, agg_z, BLOCK, agg_x, BLOCK, agg_y, BLOCK))
    expanded = shaped.reshape((2, rows, 2, count) + tuple(site_shape))
    out_re = []
    out_im = []
    for position in range(12):
        chirality = position // 6
        near_re = near_vectors[:, 0, position].astype(jnp.float32)[None]
        near_im = near_vectors[:, 1, position].astype(jnp.float32)[None]
        coarse_re = expanded[0][:, chirality]
        coarse_im = expanded[1][:, chirality]
        out_re.append(jnp.sum(near_re * coarse_re - near_im * coarse_im, axis=1))
        out_im.append(jnp.sum(near_re * coarse_im + near_im * coarse_re, axis=1))
    return jnp.stack(out_re, axis=1), jnp.stack(out_im, axis=1)


def reference(fine_solution, links, clover, near_null, coarse_links, wall_time, spin_index, wall_colour):
    extent_t, extent_z, extent_xy = fine_solution.shape[3:]
    site_shape = (extent_t, extent_z, extent_xy // NY, NY)
    links_sites = links.reshape((8, 2, 3, 3) + site_shape)
    clover_sites = clover.reshape((2, 2, 6, 6) + site_shape)
    near_sites = near_null.reshape((NVEC, 2, 12) + site_shape)
    stencil = coarse_links.reshape((9, 2, 2 * NVEC, 2 * NVEC, extent_t // BLOCK, extent_z // BLOCK,
                                    extent_xy // NY // BLOCK, NY // BLOCK))

    def single(inputs):
        solution, when, spin, colour = inputs
        folded = solution.reshape((2, 1, 4, 3) + site_shape).astype(jnp.float32)
        center = (folded[0], folded[1])
        uppers = []
        lowers = []
        for direction in range(4):
            ahead = jnp.roll(folded, -1, axis=4 + direction)
            behind = jnp.roll(folded, 1, axis=4 + direction)
            uppers.append((ahead[0], ahead[1]))
            lowers.append((behind[0], behind[1]))
        source = make_source(when[None], spin[None], colour[:, None], 0, site_shape)
        applied = wilson(center, uppers, lowers, links_sites, clover_sites)
        residual = ((source[0] - applied[0]).reshape((1, 12) + site_shape),
                    (source[1] - applied[1]).reshape((1, 12) + site_shape))
        restricted = restrict(near_sites, residual)
        estimate = restricted
        for step in range(ITERS):
            coarse_up = [jnp.roll(estimate, -1, axis=3 + direction) for direction in range(4)]
            coarse_down = [jnp.roll(estimate, 1, axis=3 + direction) for direction in range(4)]
            estimate = restricted + coarse_apply(estimate, coarse_up, coarse_down, stencil)
        correction = prolong(near_sites, estimate, site_shape)
        base = solution.astype(jnp.float32).reshape((2, 1, 12) + site_shape)
        result = base + jnp.stack(correction)
        return result.reshape((2, 12, extent_t, extent_z, extent_xy))

    mapped = lax.map(single, (jnp.moveaxis(fine_solution, 1, 0), wall_time, spin_index,
                              jnp.moveaxis(wall_colour, 1, 0)))
    return jnp.moveaxis(mapped, 0, 1)
```

```python
import jax
import jax.numpy as jnp
from jax import lax
from jax.experimental import pallas as pl
from jax.experimental.pallas import tpu as pltpu
from jax.sharding import PartitionSpec as P

BLOCK = 4
ITERS = 4
NY = 32
ROWS = 16
LANES = 128
HALF = 8
MASS = 4.1
F32 = jnp.float32
BF16 = jnp.bfloat16

gammas = [
    [[0j, 0j, 1 + 0j, 0j], [0j, 0j, 0j, 1 + 0j], [1 + 0j, 0j, 0j, 0j], [0j, 1 + 0j, 0j, 0j]],
    [[0j, 0j, 1j, 0j], [0j, 0j, 0j, -1j], [-1j, 0j, 0j, 0j], [0j, 1j, 0j, 0j]],
    [[0j, 0j, 0j, 1j], [0j, 0j, 1j, 0j], [0j, -1j, 0j, 0j], [-1j, 0j, 0j, 0j]],
    [[0j, 0j, 0j, -1 + 0j], [0j, 0j, 1 + 0j, 0j], [0j, 1 + 0j, 0j, 0j], [-1 + 0j, 0j, 0j, 0j]],
]


def vmem_params(mib):
    return pltpu.CompilerParams(vmem_limit_bytes=mib * 1024 * 1024)


def lane_index(rows):
    return lax.broadcasted_iota(jnp.int32, (rows, LANES), 1)


def row_index(rows):
    return lax.broadcasted_iota(jnp.int32, (rows, LANES), 0)


def turn_lanes(value, shift):
    return pltpu.roll(value, shift % LANES, 1)


def pack_kernel(psi_ref, t_first, t_last, z_first, z_last, x_first, x_last, stage):
    lanes = lane_index(ROWS)

    def body(component, carry):
        part = component // 12
        c = component % 12
        fields = [psi_ref[part, r, c].astype(F32) for r in range(4)]
        for r in range(4):
            stage[16 * r : 16 * r + 16, :] = fields[r]
        t_first[component] = jnp.concatenate([stage[16 * r : 16 * r + 4, :] for r in range(4)], axis=0).astype(BF16)
        t_last[component] = jnp.concatenate([stage[16 * r + 12 : 16 * r + 16, :] for r in range(4)], axis=0).astype(BF16)
        z_first[component] = stage[pl.ds(0, 16, stride=4), :].astype(BF16)
        z_last[component] = stage[pl.ds(3, 16, stride=4), :].astype(BF16)
        low = fields[0]
        high = turn_lanes(fields[0], 32)
        for r in range(1, 4):
            mask = lanes >= 32 * r
            low = jnp.where(mask, turn_lanes(fields[r], 32 * r), low)
            high = jnp.where(mask, turn_lanes(fields[r], 32 * r + 32), high)
        x_first[component] = low.astype(BF16)
        x_last[component] = high.astype(BF16)
        return carry

    lax.fori_loop(0, 24, body, 0)


def pack(psi):
    slab = jax.ShapeDtypeStruct((24, ROWS, LANES), BF16)
    vm = pl.BlockSpec(memory_space=pltpu.VMEM)
    return pl.pallas_call(
        pack_kernel,
        out_shape=(slab,) * 6,
        in_specs=[vm],
        out_specs=(vm,) * 6,
        scratch_shapes=[pltpu.VMEM((64, LANES), F32)],
        compiler_params=vmem_params(16),
    )(psi)


def times(entry, re, im):
    if entry.real != 0:
        return (entry.real, re), (entry.real, im)
    return (-entry.imag, im), (entry.imag, re)


def add_signed(total, term):
    sign, value = term
    if total is None:
        return value if sign > 0 else -value
    return total + value if sign > 0 else total - value


def fine_kernel(
    when_ref, spin_ref, offset_ref, wall_ref, psi_ref, tp_ref, tm_ref, zp_ref, zm_ref, xp_ref, xm_ref,
    links_ref, clover_ref, near_ref, out_ref, halo, shifted, text, residual, rows_ref,
):
    lanes16 = lane_index(ROWS)
    y16 = lanes16 % NY
    for which, ref in enumerate((tp_ref, tm_ref, zp_ref, zm_ref, xp_ref, xm_ref)):
        def widen(component, carry, which=which, ref=ref):
            halo[which, component] = ref[component].astype(F32)
            return carry
        lax.fori_loop(0, 24, widen, 0)

    def prepare(component, r):
        part = component // 12
        c = component % 12
        center = psi_ref[part, r, c].astype(F32)
        four = pl.multiple_of(4 * r, 4)
        text[component, 0:4, :] = halo[1, component, pl.ds(four, 4), :]
        text[component, 4:20, :] = center
        text[component, 20:24, :] = halo[0, component, pl.ds(four, 4), :]
        shifted[0, component] = center
        shifted[1, component] = pltpu.roll(center, ROWS - 1, 0)
        shifted[1, component, pl.ds(3, 4, stride=4), :] = halo[2, component, pl.ds(four, 4), :]
        shifted[2, component] = pltpu.roll(center, 1, 0)
        shifted[2, component, pl.ds(0, 4, stride=4), :] = halo[3, component, pl.ds(four, 4), :]
        above = pltpu.roll(halo[4, component], lax.rem(96 - 32 * r + LANES, LANES), 1)
        below = pltpu.roll(halo[5, component], lax.rem(LANES - 32 * r, LANES), 1)
        shifted[3, component] = jnp.where(lanes16 < 96, turn_lanes(center, -32), above)
        shifted[4, component] = jnp.where(lanes16 >= 32, turn_lanes(center, 32), below)
        shifted[5, component] = jnp.where(y16 < NY - 1, turn_lanes(center, -1), turn_lanes(center, NY - 1))
        shifted[6, component] = jnp.where(y16 > 0, turn_lanes(center, 1), turn_lanes(center, 1 - NY))

    def rhs(r, carry):
        def prep(component, inner):
            prepare(component, r)
            return inner
        lax.fori_loop(0, 24, prep, 0)
        when = when_ref[r]
        spin = spin_ref[r]
        for half in range(2):
            low = HALF * half

            def field(direction, sign, spin_in, colour, part):
                component = 12 * part + 3 * spin_in + colour
                if direction == 0:
                    start = low + 8 if sign < 0 else low
                    return text[component, start : start + HALF, :]
                which = 2 * direction - (1 if sign < 0 else 0)
                return shifted[which, component, low : low + HALF, :]

            total = [[[None, None] for _ in range(3)] for _ in range(4)]
            for direction in range(4):
                for sign in (-1.0, 1.0):
                    number = 2 * direction + (0 if sign < 0 else 1)
                    half_field = []
                    for s in range(2):
                        partner = 2 if gammas[direction][s][2] != 0 else 3
                        entry = gammas[direction][s][partner] * sign
                        row = []
                        for colour in range(3):
                            re = field(direction, sign, s, colour, 0)
                            im = field(direction, sign, s, colour, 1)
                            pre = field(direction, sign, partner, colour, 0)
                            pim = field(direction, sign, partner, colour, 1)
                            a, b = times(entry, pre, pim)
                            row.append((add_signed(re, a), add_signed(im, b)))
                        half_field.append(row)
                    for out in range(3):
                        link = [
                            (
                                links_ref[number, 0, out, inn].astype(F32)[low : low + HALF],
                                links_ref[number, 1, out, inn].astype(F32)[low : low + HALF],
                            )
                            for inn in range(3)
                        ]
                        moved = []
                        for s in range(2):
                            re = None
                            im = None
                            for inn in range(3):
                                ure, uim = link[inn]
                                hre, him = half_field[s][inn]
                                tre = ure * hre - uim * him
                                tim = ure * him + uim * hre
                                re = tre if re is None else re + tre
                                im = tim if im is None else im + tim
                            moved.append((re, im))
                        for s in range(2):
                            for part in range(2):
                                total[s][out][part] = add_signed(total[s][out][part], (1.0, moved[s][part]))
                        for s in range(2, 4):
                            source = 0 if gammas[direction][s][0] != 0 else 1
                            entry = gammas[direction][s][source] * sign
                            terms = times(entry, *moved[source])
                            for part in range(2):
                                total[s][out][part] = add_signed(total[s][out][part], terms[part])
            times_here = offset_ref[0] + 2 * half + row_index(HALF) // BLOCK
            at_wall = times_here == when
            for chirality in range(2):
                values = [
                    (
                        shifted[0, 6 * chirality + i, low : low + HALF, :],
                        shifted[0, 12 + 6 * chirality + i, low : low + HALF, :],
                    )
                    for i in range(6)
                ]
                for i in range(6):
                    re = MASS * values[i][0]
                    im = MASS * values[i][1]
                    for j in range(6):
                        cre = clover_ref[chirality, 0, i, j].astype(F32)[low : low + HALF]
                        cim = clover_ref[chirality, 1, i, j].astype(F32)[low : low + HALF]
                        re = re + (cre * values[j][0] - cim * values[j][1])
                        im = im + (cre * values[j][1] + cim * values[j][0])
                    s = 2 * chirality + i // 3
                    colour = i % 3
                    re = 0.5 * total[s][colour][0] - re
                    im = 0.5 * total[s][colour][1] - im
                    here = at_wall & (spin == s)
                    zero = jnp.zeros((HALF, LANES), F32)
                    re = re + jnp.where(here, wall_ref[r * 3 + colour], zero)
                    im = im + jnp.where(here, wall_ref[12 + r * 3 + colour], zero)
                    residual[r, 6 * chirality + i, low : low + HALF, :] = re
                    residual[r, 12 + 6 * chirality + i, low : low + HALF, :] = im
        return carry

    lax.fori_loop(0, 4, rhs, 0)

    for part in range(2):
        rows_ref[part] = jnp.zeros((LANES, LANES), F32)

    def vector(v, carry):
        for chirality in range(2):
            acc = [[None, None] for _ in range(4)]
            for c in range(6):
                position = 6 * chirality + c
                nre16 = near_ref[v, 0, position].astype(F32)
                nim16 = near_ref[v, 1, position].astype(F32)
                for half in range(2):
                    low = HALF * half
                    nre = nre16[low : low + HALF]
                    nim = nim16[low : low + HALF]
                    for r in range(4):
                        rre = residual[r, position, low : low + HALF, :]
                        rim = residual[r, 12 + position, low : low + HALF, :]
                        tre = nre * rre + nim * rim
                        tim = nre * rim - nim * rre
                        acc[r][0] = tre if acc[r][0] is None else acc[r][0] + tre
                        acc[r][1] = tim if acc[r][1] is None else acc[r][1] + tim
            for r in range(4):
                for part in range(2):
                    rows_ref[part, pl.ds(r * 32 + chirality * 12 + v, 1), :] = jnp.sum(
                        acc[r][part], axis=0, keepdims=True
                    )
        return carry

    lax.fori_loop(0, 12, vector, 0)
    member = ((lane_index(HALF) % NY) // BLOCK == row_index(HALF)).astype(F32)
    for part in range(2):
        out_ref[part] = lax.dot_general(
            member, rows_ref[part], (((1,), (1,)), ((), ())),
            precision=lax.Precision.HIGHEST, preferred_element_type=F32,
        )


def fine(wall_time, spin_index, offset, wall, psi, halos, links, clover, near):
    vm = pl.BlockSpec(memory_space=pltpu.VMEM)
    sm = pl.BlockSpec(memory_space=pltpu.SMEM)
    return pl.pallas_call(
        fine_kernel,
        out_shape=jax.ShapeDtypeStruct((2, HALF, LANES), F32),
        in_specs=[sm, sm, sm, sm] + [vm] * 10,
        out_specs=vm,
        scratch_shapes=[
            pltpu.VMEM((6, 24, ROWS, LANES), F32),
            pltpu.VMEM((7, 24, ROWS, LANES), F32),
            pltpu.VMEM((24, 24, LANES), F32),
            pltpu.VMEM((4, 24, ROWS, LANES), F32),
            pltpu.VMEM((2, LANES, LANES), F32),
        ],
        compiler_params=vmem_params(32),
    )(wall_time, spin_index, offset, wall, psi, *halos, links, clover, near)


def spread_kernel(stencil_ref, out_ref):
    def body(index, carry):
        block = stencil_ref[index]
        seg = jnp.concatenate([block, jnp.zeros((HALF, 8), F32)], axis=1)
        out_ref[index] = jnp.concatenate([seg] * 4, axis=1)
        return carry

    lax.fori_loop(0, 9 * 2 * 24, body, 0)


def spread(stencil):
    vm = pl.BlockSpec(memory_space=pltpu.VMEM)
    return pl.pallas_call(
        spread_kernel,
        out_shape=jax.ShapeDtypeStruct((9 * 2 * 24, HALF, LANES), F32),
        in_specs=[vm],
        out_specs=vm,
        compiler_params=vmem_params(16),
    )(stencil)


def merge(low, high, width, inside):
    if high is None:
        high = jnp.zeros_like(low)
    keep = jnp.where(inside, low, high)
    other = jnp.where(inside, high, low)
    return keep + jnp.where(inside, turn_lanes(other, -width), turn_lanes(other, width))


def coarse_step(estimate, neighbours, restricted_ref, operator_ref):
    members = [estimate] + neighbours
    lanes = lane_index(HALF)
    out = []
    sums = [[None] * 24, [None] * 24]
    for i in range(24):
        re = None
        im = None
        for k in range(9):
            cre = operator_ref[(k * 2) * 24 + i]
            cim = operator_ref[(k * 2 + 1) * 24 + i]
            ere, eim = members[k]
            tre = cre * ere - cim * eim
            tim = cre * eim + cim * ere
            re = tre if re is None else re + tre
            im = tim if im is None else im + tim
        sums[0][i] = re
        sums[1][i] = im
    for part in range(2):
        values = sums[part] + [None] * 8
        width = 16
        while width >= 1:
            inside = (lanes // width) % 2 == 0
            count = width
            values = [
                None if values[i] is None else merge(values[i], values[i + count], width, inside)
                for i in range(count)
            ]
            width //= 2
        out.append(restricted_ref[part] + values[0])
    return out


def coarse_neighbours(estimate, refs):
    neighbours = [(ref[0], ref[1]) for ref in refs]
    neighbours.append(tuple(pltpu.roll(value, HALF - 1, 0) for value in estimate))
    neighbours.append(tuple(pltpu.roll(value, 1, 0) for value in estimate))
    return neighbours


def coarse_kernel(e_ref, tp, tm, zp, zm, xp, xm, r_ref, operator_ref, out_ref):
    estimate = (e_ref[0], e_ref[1])
    out = coarse_step(estimate, coarse_neighbours(estimate, (tp, tm, zp, zm, xp, xm)), r_ref, operator_ref)
    out_ref[0] = out[0]
    out_ref[1] = out[1]


def coarse(estimate, halos, restricted, operator):
    vm = pl.BlockSpec(memory_space=pltpu.VMEM)
    return pl.pallas_call(
        coarse_kernel,
        out_shape=jax.ShapeDtypeStruct((2, HALF, LANES), F32),
        in_specs=[vm] * 9,
        out_specs=vm,
        compiler_params=vmem_params(16),
    )(estimate, *halos, restricted, operator)


def last_kernel(e_ref, tp, tm, zp, zm, xp, xm, r_ref, operator_ref, psi_ref, near_ref, out_ref, wide):
    estimate = (e_ref[0], e_ref[1])
    final = coarse_step(estimate, coarse_neighbours(estimate, (tp, tm, zp, zm, xp, xm)), r_ref, operator_ref)
    member = ((lane_index(HALF) % NY) // BLOCK == row_index(HALF)).astype(F32)
    for part in range(2):
        wide[part] = lax.dot_general(
            final[part], member, (((0,), (0,)), ((), ())),
            precision=lax.Precision.HIGHEST, preferred_element_type=F32,
        )

    def component(c, carry):
        base = (c // 6) * 12
        near = [(near_ref[v, 0, c].astype(F32), near_ref[v, 1, c].astype(F32)) for v in range(12)]
        for r in range(4):
            re = psi_ref[0, r, c].astype(F32)
            im = psi_ref[1, r, c].astype(F32)
            for v in range(12):
                ere = wide[0, pl.ds(r * 32 + base + v, 1), :]
                eim = wide[1, pl.ds(r * 32 + base + v, 1), :]
                nre, nim = near[v]
                re = re + (nre * ere - nim * eim)
                im = im + (nre * eim + nim * ere)
            out_ref[0, r, c] = re
            out_ref[1, r, c] = im
        return carry

    lax.fori_loop(0, 12, component, 0)


def last(estimate, halos, restricted, operator, psi, near):
    vm = pl.BlockSpec(memory_space=pltpu.VMEM)
    return pl.pallas_call(
        last_kernel,
        out_shape=jax.ShapeDtypeStruct((2, 4, 12, ROWS, LANES), F32),
        in_specs=[vm] * 11,
        out_specs=vm,
        scratch_shapes=[pltpu.VMEM((2, LANES, LANES), F32)],
        compiler_params=vmem_params(24),
    )(estimate, *halos, restricted, operator, psi, near)


def send(value, axis, step):
    count = lax.axis_size(axis)
    return lax.ppermute(value, axis, [(i, (i + step) % count) for i in range(count)])


def exchange(value):
    halos = []
    for axis in ("ta", "gz", "xy"):
        halos.append(send(value, axis, -1))
        halos.append(send(value, axis, 1))
    return halos


def local(
    fine_solution, links, clover, near_null, coarse_links, wall_time, spin_index, wall_colour
):
    psi = fine_solution.reshape((2, 4, 12, ROWS, LANES))
    links = links.reshape((8, 2, 3, 3, ROWS, LANES))
    clover = clover.reshape((2, 2, 6, 6, ROWS, LANES))
    near = near_null.reshape((12, 2, 12, ROWS, LANES))
    stencil = jnp.transpose(coarse_links, (0, 1, 2, 4, 5, 6, 3)).reshape((9 * 2 * 24, HALF, 24))
    wall = wall_colour.reshape((24,))
    offset = (lax.axis_index("ta") * 4).astype(jnp.int32).reshape((1,))
    t_first, t_last, z_first, z_last, x_first, x_last = pack(psi)
    halos = [
        send(t_first, "ta", -1),
        send(t_last, "ta", 1),
        send(z_first, "gz", -1),
        send(z_last, "gz", 1),
        send(x_first, "xy", -1),
        send(x_last, "xy", 1),
    ]
    operator = spread(stencil)
    restricted = fine(wall_time, spin_index, offset, wall, psi, halos, links, clover, near)
    estimate = restricted
    for step in range(ITERS - 1):
        estimate = coarse(estimate, exchange(estimate), restricted, operator)
    result = last(estimate, exchange(estimate), restricted, operator, psi, near)
    return result.reshape(fine_solution.shape)


def solution(mesh):
    placed = (
        P(None, None, None, "ta", "gz", "xy"),
        P(None, None, None, None, "ta", "gz", "xy"),
        P(None, None, None, None, "ta", "gz", "xy"),
        P(None, None, None, "ta", "gz", "xy"),
        P(None, None, None, None, "ta", "gz", "xy"),
        P(),
        P(),
        P(),
    )
    return jax.shard_map(
        local,
        mesh=mesh,
        in_specs=placed,
        out_specs=P(None, None, None, "ta", "gz", "xy"),
        check_vma=False,
    )
```

```python
import jax
import jax.numpy as jnp
from jax import lax
from jax.experimental import pallas as pl
from jax.experimental.pallas import tpu as pltpu
from jax.sharding import PartitionSpec as P

BLOCK = 4
ITERS = 4
NY = 32
ROWS = 16
LANES = 128
HALF = 8
MASS = 4.1
F32 = jnp.float32
BF16 = jnp.bfloat16

gammas = [
    [[0j, 0j, 1 + 0j, 0j], [0j, 0j, 0j, 1 + 0j], [1 + 0j, 0j, 0j, 0j], [0j, 1 + 0j, 0j, 0j]],
    [[0j, 0j, 1j, 0j], [0j, 0j, 0j, -1j], [-1j, 0j, 0j, 0j], [0j, 1j, 0j, 0j]],
    [[0j, 0j, 0j, 1j], [0j, 0j, 1j, 0j], [0j, -1j, 0j, 0j], [-1j, 0j, 0j, 0j]],
    [[0j, 0j, 0j, -1 + 0j], [0j, 0j, 1 + 0j, 0j], [0j, 1 + 0j, 0j, 0j], [-1 + 0j, 0j, 0j, 0j]],
]


def vmem_params(mib):
    return pltpu.CompilerParams(vmem_limit_bytes=mib * 1024 * 1024)


def lane_index(rows):
    return lax.broadcasted_iota(jnp.int32, (rows, LANES), 1)


def row_index(rows):
    return lax.broadcasted_iota(jnp.int32, (rows, LANES), 0)


def turn_lanes(value, shift):
    return pltpu.roll(value, shift % LANES, 1)


def swap(value, axis, matching):
    count = lax.axis_size(axis)
    if matching == 0:
        pairs = [(i, i ^ 1) for i in range(count)]
    else:
        pairs = [(i, (i + 1 if i % 2 else i - 1) % count) for i in range(count)]
    return lax.ppermute(value, axis, pairs)


def is_even(axis):
    return lax.rem(lax.axis_index(axis), 2) == 0


def pack_kernel(psi_ref, ta_ref, tb_ref, za_ref, zb_ref, xa_ref, xb_ref, wide_ref):
    lanes = lane_index(ROWS)
    even = [is_even(axis) for axis in ("ta", "gz", "xy")]

    def store(component, which, first, last):
        toward_a, toward_b = ((ta_ref, tb_ref), (za_ref, zb_ref), (xa_ref, xb_ref))[which]
        toward_a[component] = jnp.where(even[which], last, first).astype(BF16)
        toward_b[component] = jnp.where(even[which], first, last).astype(BF16)

    def body(component, carry):
        part = component // 12
        c = component % 12
        fields = [psi_ref[part, r, c].astype(F32) for r in range(4)]
        for r in range(4):
            wide_ref[part, r, c] = fields[r]
        store(
            component, 0,
            jnp.concatenate([wide_ref[part, r, c, 0:4, :] for r in range(4)], axis=0),
            jnp.concatenate([wide_ref[part, r, c, 12:16, :] for r in range(4)], axis=0),
        )
        store(
            component, 1,
            jnp.concatenate([wide_ref[part, r, c, pl.ds(0, 4, stride=4), :] for r in range(4)], axis=0),
            jnp.concatenate([wide_ref[part, r, c, pl.ds(3, 4, stride=4), :] for r in range(4)], axis=0),
        )
        low = fields[0]
        high = turn_lanes(fields[0], 32)
        for r in range(1, 4):
            mask = lanes >= 32 * r
            low = jnp.where(mask, turn_lanes(fields[r], 32 * r), low)
            high = jnp.where(mask, turn_lanes(fields[r], 32 * r + 32), high)
        store(component, 2, low, high)
        return carry

    lax.fori_loop(0, 24, body, 0, unroll=4)


def pack(psi):
    slab = jax.ShapeDtypeStruct((24, ROWS, LANES), BF16)
    wide = jax.ShapeDtypeStruct((2, 4, 12, ROWS, LANES), F32)
    vm = pl.BlockSpec(memory_space=pltpu.VMEM)
    return pl.pallas_call(
        pack_kernel,
        out_shape=(slab,) * 6 + (wide,),
        in_specs=[vm],
        out_specs=(vm,) * 7,
        compiler_params=vmem_params(16),
    )(psi)


def times(entry, re, im):
    if entry.real != 0:
        return (entry.real, re), (entry.real, im)
    return (-entry.imag, im), (entry.imag, re)


def add_signed(total, term):
    sign, value = term
    if total is None:
        return value if sign > 0 else -value
    return total + value if sign > 0 else total - value


def projected(direction, sign, load):
    rows = []
    for s in range(2):
        partner = 2 if gammas[direction][s][2] != 0 else 3
        entry = gammas[direction][s][partner] * sign
        row = []
        for colour in range(3):
            a, b = times(entry, load(0, 3 * partner + colour), load(1, 3 * partner + colour))
            row.append((
                add_signed(load(0, 3 * s + colour), a),
                add_signed(load(1, 3 * s + colour), b),
            ))
        rows.append(row)
    return rows


def mapped(function, *tables):
    return [
        [
            tuple(function(*[table[s][colour][part] for table in tables]) for part in range(2))
            for colour in range(3)
        ]
        for s in range(2)
    ]


def hop(direction, sign, half_field, link, total):
    for out in range(3):
        row = [link(0, out, inn) for inn in range(3)], [link(1, out, inn) for inn in range(3)]
        moved = []
        for s in range(2):
            re = None
            im = None
            for inn in range(3):
                ure, uim = row[0][inn], row[1][inn]
                hre, him = half_field[s][inn]
                tre = ure * hre - uim * him
                tim = ure * him + uim * hre
                re = tre if re is None else re + tre
                im = tim if im is None else im + tim
            moved.append((re, im))
        for s in range(2):
            for part in range(2):
                total[s][out][part] = add_signed(total[s][out][part], (1.0, moved[s][part]))
        for s in range(2, 4):
            source = 0 if gammas[direction][s][0] != 0 else 1
            entry = gammas[direction][s][source] * sign
            terms = times(entry, *moved[source])
            for part in range(2):
                total[s][out][part] = add_signed(total[s][out][part], terms[part])


def link_loader(links_ref, number, low):
    def link(part, out, inn):
        return links_ref[number, part, out, inn].astype(F32)[low : low + HALF]
    return link


def centre_kernel(
    wide_ref, when_hbm, spin_hbm, wall_hbm, links_hbm, clover_hbm, stencil_hbm, out_ref, operator_ref,
    when_ref, spin_ref, wall_ref, links_ref, clover_ref, stencil_ref, sems,
):
    copies = [
        pltpu.make_async_copy(source, target, sems.at[i])
        for i, (source, target) in enumerate((
            (when_hbm, when_ref), (spin_hbm, spin_ref), (wall_hbm, wall_ref),
            (links_hbm.at[pl.ds(6, 2)], links_ref), (clover_hbm, clover_ref), (stencil_hbm, stencil_ref),
        ))
    ]
    for copy in copies:
        copy.start()
    for copy in copies[:5]:
        copy.wait()
    lanes = lane_index(HALF)
    y = lanes % NY
    first_time = lax.axis_index("ta") * BLOCK

    def rhs(r, carry):
        when = when_ref[r]
        spin = spin_ref[r]
        for half in range(2):
            low = HALF * half

            def load(part, component):
                return wide_ref[part, r, component, low : low + HALF, :]

            total = [[[None, None] for _ in range(3)] for _ in range(4)]
            ahead = mapped(
                lambda p: jnp.where(y < NY - 1, turn_lanes(p, -1), turn_lanes(p, NY - 1)),
                projected(3, -1.0, load),
            )
            hop(3, -1.0, ahead, link_loader(links_ref, 0, low), total)
            behind = mapped(
                lambda p: jnp.where(y > 0, turn_lanes(p, 1), turn_lanes(p, 1 - NY)),
                projected(3, 1.0, load),
            )
            hop(3, 1.0, behind, link_loader(links_ref, 1, low), total)
            at_wall = first_time + 2 * half + row_index(HALF) // BLOCK == when
            for chirality in range(2):
                values = [(load(0, 6 * chirality + i), load(1, 6 * chirality + i)) for i in range(6)]
                for i in range(6):
                    re = MASS * values[i][0]
                    im = MASS * values[i][1]
                    for j in range(6):
                        cre = clover_ref[chirality, 0, i, j].astype(F32)[low : low + HALF]
                        cim = clover_ref[chirality, 1, i, j].astype(F32)[low : low + HALF]
                        re = re + (cre * values[j][0] - cim * values[j][1])
                        im = im + (cre * values[j][1] + cim * values[j][0])
                    s = 2 * chirality + i // 3
                    colour = i % 3
                    here = spin == s
                    sre = jnp.where(here, wall_ref[colour, 0, r], 0.0)
                    sim = jnp.where(here, wall_ref[colour, 1, r], 0.0)
                    re = jnp.where(at_wall, sre, 0.0) + (0.5 * total[s][colour][0] - re)
                    im = jnp.where(at_wall, sim, 0.0) + (0.5 * total[s][colour][1] - im)
                    out_ref[r, 6 * chirality + i, low : low + HALF, :] = re
                    out_ref[r, 12 + 6 * chirality + i, low : low + HALF, :] = im
        return carry

    lax.fori_loop(0, 4, rhs, 0)
    copies[5].wait()

    def spread(index, carry):
        start = pl.multiple_of(24 * index, 24)
        block = stencil_ref[pl.ds(start, 24)].reshape((24 * HALF, 24))
        block = jnp.concatenate([block, jnp.zeros((24 * HALF, LANES - 24), F32)], axis=1)
        block = block + turn_lanes(block, 32)
        block = block + turn_lanes(block, 64)
        operator_ref[pl.ds(start, 24)] = block.reshape((24, HALF, LANES))
        return carry

    lax.fori_loop(0, 18, spread, 0)


def centre(wide, wall_time, spin_index, wall, links, clover, stencil):
    vm = pl.BlockSpec(memory_space=pltpu.VMEM)
    hbm = pl.BlockSpec(memory_space=pltpu.HBM)
    return pl.pallas_call(
        centre_kernel,
        out_shape=(
            jax.ShapeDtypeStruct((4, 24, ROWS, LANES), F32),
            jax.ShapeDtypeStruct((9 * 2 * 24, HALF, LANES), F32),
        ),
        in_specs=[vm] + [hbm] * 6,
        out_specs=(vm, vm),
        scratch_shapes=[
            pltpu.SMEM((4,), jnp.int32),
            pltpu.SMEM((4,), jnp.int32),
            pltpu.SMEM((3, 2, 4), F32),
            pltpu.VMEM((2, 2, 3, 3, ROWS, LANES), BF16),
            pltpu.VMEM((2, 2, 6, 6, ROWS, LANES), BF16),
            pltpu.VMEM((9 * 2 * 24, HALF, 24), F32),
            pltpu.SemaphoreType.DMA((6,)),
        ],
        compiler_params=vmem_params(24),
        cost_estimate=pl.CostEstimate(flops=40_000_000, bytes_accessed=6_000_000, transcendentals=0),
    )(wide, wall_time, spin_index, wall, links, clover, stencil)


def fine_kernel(
    wide_ref, partial_ref, ta_ref, tb_ref, za_ref, zb_ref, xa_ref, xb_ref, links_hbm, near_hbm,
    out_ref, links_ref, near_ref, tedge, zedge, xedge, residual, rows_ref, sems,
):
    links_copy = pltpu.make_async_copy(links_hbm.at[pl.ds(0, 6)], links_ref, sems.at[0])
    near_copy = pltpu.make_async_copy(near_hbm, near_ref, sems.at[1])
    links_copy.start()
    near_copy.start()
    even = [is_even(axis) for axis in ("ta", "gz", "xy")]
    slabs = ((ta_ref, tb_ref), (za_ref, zb_ref), (xa_ref, xb_ref))
    for direction in range(3):
        for side, sign in enumerate((-1.0, 1.0)):
            toward_a, toward_b = slabs[direction]

            def load(part, component):
                a = toward_a[12 * part + component].astype(F32)
                b = toward_b[12 * part + component].astype(F32)
                return jnp.where(even[direction], a, b) if side == 0 else jnp.where(even[direction], b, a)

            edge = projected(direction, sign, load)
            for s in range(2):
                for colour in range(3):
                    for part in range(2):
                        slot = 6 * s + 2 * colour + part
                        value = edge[s][colour][part]
                        if direction == 0:
                            for r in range(4):
                                tedge[side, slot, r, 0:4, :] = value[4 * r : 4 * r + 4]
                                tedge[side, slot, r, 4:8, :] = value[4 * r : 4 * r + 4]
                        elif direction == 1:
                            zedge[side, slot] = value
                        else:
                            xedge[side, slot] = value
    links_copy.wait()
    lanes = lane_index(HALF)
    sub = row_index(HALF)
    upper = sub >= 4
    z = sub % BLOCK

    def rhs(r, carry):
        def table(read):
            return [[tuple(read(6 * s + 2 * colour + part) for part in range(2)) for colour in range(3)] for s in range(2)]

        for half in range(2):
            low = HALF * half

            def loader(start):
                def load(part, component):
                    return wide_ref[part, r, component, start : start + HALF, :]
                return load

            total = [[[None, None] for _ in range(3)] for _ in range(4)]
            for side, sign in enumerate((-1.0, 1.0)):
                def turned(start):
                    return mapped(lambda p: pltpu.roll(p, 4, 0), projected(0, sign, loader(start)))

                edge = table(lambda slot: tedge[side, slot, r])
                if side == 0:
                    lower_part, upper_part = (turned(0), turned(8)) if half == 0 else (turned(8), edge)
                else:
                    lower_part, upper_part = (edge, turned(0)) if half == 0 else (turned(0), turned(8))
                field = mapped(lambda a, b: jnp.where(upper, b, a), lower_part, upper_part)
                hop(0, sign, field, link_loader(links_ref, side, low), total)
            for side, sign in enumerate((-1.0, 1.0)):
                row = 4 * r + 2 * half
                first = table(lambda slot: zedge[side, slot, pl.ds(row, 1), :])
                second = table(lambda slot: zedge[side, slot, pl.ds(row + 1, 1), :])
                shift, place = (HALF - 1, 3) if side == 0 else (1, 0)
                field = mapped(
                    lambda p, a, b: jnp.where(z == place, jnp.where(upper, b, a), pltpu.roll(p, shift, 0)),
                    projected(1, sign, loader(low)), first, second,
                )
                hop(1, sign, field, link_loader(links_ref, 2 + side, low), total)
            for side, sign in enumerate((-1.0, 1.0)):
                edge = table(lambda slot: xedge[side, slot, low : low + HALF, :])
                if side == 0:
                    inside = lanes < 96
                    amount = lax.rem(96 - 32 * r + LANES, LANES)
                    shift = LANES - 32
                else:
                    inside = lanes >= 32
                    amount = lax.rem(LANES - 32 * r, LANES)
                    shift = 32
                field = mapped(
                    lambda p, e: jnp.where(inside, pltpu.roll(p, shift, 1), pltpu.roll(e, amount, 1)),
                    projected(2, sign, loader(low)), edge,
                )
                hop(2, sign, field, link_loader(links_ref, 4 + side, low), total)
            for s in range(4):
                for colour in range(3):
                    for part in range(2):
                        position = 12 * part + 3 * s + colour
                        residual[r, position, low : low + HALF, :] = (
                            partial_ref[r, position, low : low + HALF, :] + 0.5 * total[s][colour][part]
                        )
        return carry

    lax.fori_loop(0, 4, rhs, 0)

    for part in range(2):
        rows_ref[part] = jnp.zeros((LANES, LANES), F32)
    near_copy.wait()

    def vector(v, carry):
        for chirality in range(2):
            acc = [[None, None] for _ in range(4)]
            for c in range(6):
                position = 6 * chirality + c
                nre16 = near_ref[v, 0, position].astype(F32)
                nim16 = near_ref[v, 1, position].astype(F32)
                for half in range(2):
                    low = HALF * half
                    nre = nre16[low : low + HALF]
                    nim = nim16[low : low + HALF]
                    for r in range(4):
                        rre = residual[r, position, low : low + HALF, :]
                        rim = residual[r, 12 + position, low : low + HALF, :]
                        tre = nre * rre + nim * rim
                        tim = nre * rim - nim * rre
                        acc[r][0] = tre if acc[r][0] is None else acc[r][0] + tre
                        acc[r][1] = tim if acc[r][1] is None else acc[r][1] + tim
            for r in range(4):
                for part in range(2):
                    rows_ref[part, pl.ds(r * 32 + chirality * 12 + v, 1), :] = jnp.sum(
                        acc[r][part], axis=0, keepdims=True
                    )
        return carry

    lax.fori_loop(0, 12, vector, 0)
    member = ((lane_index(HALF) % NY) // BLOCK == row_index(HALF)).astype(F32)
    for part in range(2):
        out_ref[part] = lax.dot_general(
            member, rows_ref[part], (((1,), (1,)), ((), ())),
            precision=lax.Precision.HIGHEST, preferred_element_type=F32,
        )


def fine(wide, partial, halos, links, near):
    vm = pl.BlockSpec(memory_space=pltpu.VMEM)
    hbm = pl.BlockSpec(memory_space=pltpu.HBM)
    return pl.pallas_call(
        fine_kernel,
        out_shape=jax.ShapeDtypeStruct((2, HALF, LANES), F32),
        in_specs=[vm] * 8 + [hbm] * 2,
        out_specs=vm,
        scratch_shapes=[
            pltpu.VMEM((6, 2, 3, 3, ROWS, LANES), BF16),
            pltpu.VMEM((12, 2, 12, ROWS, LANES), BF16),
            pltpu.VMEM((2, 12, 4, HALF, LANES), F32),
            pltpu.VMEM((2, 12, ROWS, LANES), F32),
            pltpu.VMEM((2, 12, ROWS, LANES), F32),
            pltpu.VMEM((4, 24, ROWS, LANES), F32),
            pltpu.VMEM((2, LANES, LANES), F32),
            pltpu.SemaphoreType.DMA((2,)),
        ],
        compiler_params=vmem_params(24),
    )(wide, partial, *halos, links, near)


def merge(low, high, width, inside):
    if high is None:
        high = jnp.zeros_like(low)
    keep = jnp.where(inside, low, high)
    other = jnp.where(inside, high, low)
    return keep + jnp.where(inside, turn_lanes(other, -width), turn_lanes(other, width))


def coarse_step(estimate, neighbours, restricted_ref, operator_ref):
    members = [estimate] + neighbours
    lanes = lane_index(HALF)
    out = []
    sums = [[None] * 24, [None] * 24]
    for i in range(24):
        re = None
        im = None
        for k in range(9):
            cre = operator_ref[(k * 2) * 24 + i]
            cim = operator_ref[(k * 2 + 1) * 24 + i]
            ere, eim = members[k]
            tre = cre * ere - cim * eim
            tim = cre * eim + cim * ere
            re = tre if re is None else re + tre
            im = tim if im is None else im + tim
        sums[0][i] = re
        sums[1][i] = im
    for part in range(2):
        values = sums[part] + [None] * 8
        width = 16
        while width >= 1:
            inside = (lanes // width) % 2 == 0
            count = width
            values = [
                None if values[i] is None else merge(values[i], values[i + count], width, inside)
                for i in range(count)
            ]
            width //= 2
        out.append(restricted_ref[part] + values[0])
    return out


def coarse_neighbours(estimate, refs):
    neighbours = []
    for direction, axis in enumerate(("ta", "gz", "xy")):
        even = is_even(axis)
        a = refs[2 * direction]
        b = refs[2 * direction + 1]
        neighbours.append(tuple(jnp.where(even, a[part], b[part]) for part in range(2)))
        neighbours.append(tuple(jnp.where(even, b[part], a[part]) for part in range(2)))
    neighbours.append(tuple(pltpu.roll(value, HALF - 1, 0) for value in estimate))
    neighbours.append(tuple(pltpu.roll(value, 1, 0) for value in estimate))
    return neighbours


def coarse_kernel(e_ref, tp, tm, zp, zm, xp, xm, r_ref, operator_ref, out_ref):
    estimate = (e_ref[0], e_ref[1])
    out = coarse_step(estimate, coarse_neighbours(estimate, (tp, tm, zp, zm, xp, xm)), r_ref, operator_ref)
    out_ref[0] = out[0]
    out_ref[1] = out[1]


def coarse(estimate, halos, restricted, operator):
    vm = pl.BlockSpec(memory_space=pltpu.VMEM)
    return pl.pallas_call(
        coarse_kernel,
        out_shape=jax.ShapeDtypeStruct((2, HALF, LANES), F32),
        in_specs=[vm] * 9,
        out_specs=vm,
        compiler_params=vmem_params(16),
    )(estimate, *halos, restricted, operator)


def last_kernel(e_ref, tp, tm, zp, zm, xp, xm, r_ref, operator_ref, psi_ref, near_ref, out_ref, wide):
    estimate = (e_ref[0], e_ref[1])
    final = coarse_step(estimate, coarse_neighbours(estimate, (tp, tm, zp, zm, xp, xm)), r_ref, operator_ref)
    member = ((lane_index(HALF) % NY) // BLOCK == row_index(HALF)).astype(F32)
    for part in range(2):
        wide[part] = lax.dot_general(
            final[part], member, (((0,), (0,)), ((), ())),
            precision=lax.Precision.HIGHEST, preferred_element_type=F32,
        )

    def component(c, carry):
        base = (c // 6) * 12
        near = [(near_ref[v, 0, c].astype(F32), near_ref[v, 1, c].astype(F32)) for v in range(12)]
        for r in range(4):
            re = psi_ref[0, r, c]
            im = psi_ref[1, r, c]
            for v in range(12):
                ere = wide[0, pl.ds(r * 32 + base + v, 1), :]
                eim = wide[1, pl.ds(r * 32 + base + v, 1), :]
                nre, nim = near[v]
                re = re + (nre * ere - nim * eim)
                im = im + (nre * eim + nim * ere)
            out_ref[0, r, c] = re
            out_ref[1, r, c] = im
        return carry

    lax.fori_loop(0, 12, component, 0)


def last(estimate, halos, restricted, operator, psi, near):
    vm = pl.BlockSpec(memory_space=pltpu.VMEM)
    return pl.pallas_call(
        last_kernel,
        out_shape=jax.ShapeDtypeStruct((2, 4, 12, ROWS, LANES), F32),
        in_specs=[vm] * 11,
        out_specs=vm,
        scratch_shapes=[pltpu.VMEM((2, LANES, LANES), F32)],
        compiler_params=vmem_params(24),
    )(estimate, *halos, restricted, operator, psi, near)


def exchange(values):
    return [
        swap(value, axis, which % 2)
        for which, (value, axis) in enumerate(zip(values, ("ta", "ta", "gz", "gz", "xy", "xy")))
    ]


def local(
    fine_solution, links, clover, near_null, coarse_links, wall_time, spin_index, wall_colour
):
    psi = fine_solution.reshape((2, 4, 12, ROWS, LANES))
    links = links.reshape((8, 2, 3, 3, ROWS, LANES))
    clover = clover.reshape((2, 2, 6, 6, ROWS, LANES))
    near = near_null.reshape((12, 2, 12, ROWS, LANES))
    stencil = jnp.transpose(coarse_links, (0, 1, 2, 4, 5, 6, 3)).reshape((9 * 2 * 24, HALF, 24))
    wall = jnp.transpose(wall_colour, (2, 0, 1))
    *slabs, wide = pack(psi)
    halos = exchange(slabs)
    partial, operator = centre(wide, wall_time, spin_index, wall, links, clover, stencil)
    restricted = fine(wide, partial, halos, links, near)
    estimate = restricted
    for step in range(ITERS - 1):
        estimate = coarse(estimate, exchange([estimate] * 6), restricted, operator)
    result = last(estimate, exchange([estimate] * 6), restricted, operator, wide, near)
    return result.reshape(fine_solution.shape)


def solution(mesh):
    placed = (
        P(None, None, None, "ta", "gz", "xy"),
        P(None, None, None, None, "ta", "gz", "xy"),
        P(None, None, None, None, "ta", "gz", "xy"),
        P(None, None, None, "ta", "gz", "xy"),
        P(None, None, None, None, "ta", "gz", "xy"),
        P(),
        P(),
        P(),
    )
    return jax.shard_map(
        local,
        mesh=mesh,
        in_specs=placed,
        out_specs=P(None, None, None, "ta", "gz", "xy"),
        check_vma=False,
    )
```

```python
import jax
import jax.numpy as jnp
from jax import lax
from jax.experimental import pallas as pl
from jax.experimental.pallas import tpu as pltpu
from jax.sharding import PartitionSpec as P

BLOCK = 4
ITERS = 4
NY = 32
ROWS = 16
LANES = 128
HALF = 8
MASS = 4.1
F32 = jnp.float32
BF16 = jnp.bfloat16

gammas = [
    [[0j, 0j, 1 + 0j, 0j], [0j, 0j, 0j, 1 + 0j], [1 + 0j, 0j, 0j, 0j], [0j, 1 + 0j, 0j, 0j]],
    [[0j, 0j, 1j, 0j], [0j, 0j, 0j, -1j], [-1j, 0j, 0j, 0j], [0j, 1j, 0j, 0j]],
    [[0j, 0j, 0j, 1j], [0j, 0j, 1j, 0j], [0j, -1j, 0j, 0j], [-1j, 0j, 0j, 0j]],
    [[0j, 0j, 0j, -1 + 0j], [0j, 0j, 1 + 0j, 0j], [0j, 1 + 0j, 0j, 0j], [-1 + 0j, 0j, 0j, 0j]],
]


def vmem_params(mib):
    return pltpu.CompilerParams(vmem_limit_bytes=mib * 1024 * 1024)


def lane_index(rows):
    return lax.broadcasted_iota(jnp.int32, (rows, LANES), 1)


def row_index(rows):
    return lax.broadcasted_iota(jnp.int32, (rows, LANES), 0)


def turn_lanes(value, shift):
    return pltpu.roll(value, shift % LANES, 1)


def swap(value, axis, matching):
    count = lax.axis_size(axis)
    if matching == 0:
        pairs = [(i, i ^ 1) for i in range(count)]
    else:
        pairs = [(i, (i + 1 if i % 2 else i - 1) % count) for i in range(count)]
    return lax.ppermute(value, axis, pairs)


def is_even(axis):
    return lax.rem(lax.axis_index(axis), 2) == 0


def pack_kernel(psi_ref, ta_ref, tb_ref, za_ref, zb_ref, xa_ref, xb_ref, wide_ref):
    lanes = lane_index(ROWS)
    even = [is_even(axis) for axis in ("ta", "gz", "xy")]

    def store(component, which, first, last):
        toward_a, toward_b = ((ta_ref, tb_ref), (za_ref, zb_ref), (xa_ref, xb_ref))[which]
        toward_a[component] = jnp.where(even[which], last, first).astype(BF16)
        toward_b[component] = jnp.where(even[which], first, last).astype(BF16)

    def body(component, carry):
        part = component // 12
        c = component % 12
        fields = [psi_ref[part, r, c].astype(F32) for r in range(4)]
        for r in range(4):
            wide_ref[part, r, c] = fields[r]
        store(
            component, 0,
            jnp.concatenate([wide_ref[part, r, c, 0:4, :] for r in range(4)], axis=0),
            jnp.concatenate([wide_ref[part, r, c, 12:16, :] for r in range(4)], axis=0),
        )
        store(
            component, 1,
            jnp.concatenate([wide_ref[part, r, c, pl.ds(0, 4, stride=4), :] for r in range(4)], axis=0),
            jnp.concatenate([wide_ref[part, r, c, pl.ds(3, 4, stride=4), :] for r in range(4)], axis=0),
        )
        low = fields[0]
        high = turn_lanes(fields[0], 32)
        for r in range(1, 4):
            mask = lanes >= 32 * r
            low = jnp.where(mask, turn_lanes(fields[r], 32 * r), low)
            high = jnp.where(mask, turn_lanes(fields[r], 32 * r + 32), high)
        store(component, 2, low, high)
        return carry

    lax.fori_loop(0, 24, body, 0, unroll=4)


def pack(psi):
    slab = jax.ShapeDtypeStruct((24, ROWS, LANES), BF16)
    wide = jax.ShapeDtypeStruct((2, 4, 12, ROWS, LANES), F32)
    vm = pl.BlockSpec(memory_space=pltpu.VMEM)
    return pl.pallas_call(
        pack_kernel,
        out_shape=(slab,) * 6 + (wide,),
        in_specs=[vm],
        out_specs=(vm,) * 7,
        compiler_params=vmem_params(16),
        cost_estimate=pl.CostEstimate(flops=40_000_000, bytes_accessed=40_000_000, transcendentals=0),
    )(psi)


def times(entry, re, im):
    if entry.real != 0:
        return (entry.real, re), (entry.real, im)
    return (-entry.imag, im), (entry.imag, re)


def add_signed(total, term):
    sign, value = term
    if total is None:
        return value if sign > 0 else -value
    return total + value if sign > 0 else total - value


def projected(direction, sign, load):
    rows = []
    for s in range(2):
        partner = 2 if gammas[direction][s][2] != 0 else 3
        entry = gammas[direction][s][partner] * sign
        row = []
        for colour in range(3):
            a, b = times(entry, load(0, 3 * partner + colour), load(1, 3 * partner + colour))
            row.append((
                add_signed(load(0, 3 * s + colour), a),
                add_signed(load(1, 3 * s + colour), b),
            ))
        rows.append(row)
    return rows


def mapped(function, *tables):
    return [
        [
            tuple(function(*[table[s][colour][part] for table in tables]) for part in range(2))
            for colour in range(3)
        ]
        for s in range(2)
    ]


def hop(direction, sign, half_field, link, total):
    for out in range(3):
        row = [link(0, out, inn) for inn in range(3)], [link(1, out, inn) for inn in range(3)]
        moved = []
        for s in range(2):
            re = None
            im = None
            for inn in range(3):
                ure, uim = row[0][inn], row[1][inn]
                hre, him = half_field[s][inn]
                tre = ure * hre - uim * him
                tim = ure * him + uim * hre
                re = tre if re is None else re + tre
                im = tim if im is None else im + tim
            moved.append((re, im))
        for s in range(2):
            for part in range(2):
                total[s][out][part] = add_signed(total[s][out][part], (1.0, moved[s][part]))
        for s in range(2, 4):
            source = 0 if gammas[direction][s][0] != 0 else 1
            entry = gammas[direction][s][source] * sign
            terms = times(entry, *moved[source])
            for part in range(2):
                total[s][out][part] = add_signed(total[s][out][part], terms[part])


def link_loader(links_ref, number, low):
    def link(part, out, inn):
        return links_ref[number, part, out, inn].astype(F32)[low : low + HALF]
    return link


def centre_kernel(
    wide_ref, when_hbm, spin_hbm, wall_hbm, links_hbm, clover_hbm, stencil_hbm, out_ref, operator_ref,
    links_ref, clover_ref, stencil_ref, when_ref, spin_ref, wall_ref, sems,
):
    copies = [
        pltpu.make_async_copy(source, target, sems.at[i])
        for i, (source, target) in enumerate((
            (links_hbm.at[pl.ds(6, 2)], links_ref), (clover_hbm, clover_ref), (stencil_hbm, stencil_ref),
            (when_hbm, when_ref), (spin_hbm, spin_ref), (wall_hbm, wall_ref),
        ))
    ]
    for copy in copies:
        copy.start()
    for copy in copies:
        copy.wait()
    lanes = lane_index(HALF)
    y = lanes % NY
    first_time = lax.axis_index("ta") * BLOCK

    def rhs(r, carry):
        when = when_ref[r]
        spin = spin_ref[r]
        for half in range(2):
            low = HALF * half

            def load(part, component):
                return wide_ref[part, r, component, low : low + HALF, :]

            total = [[[None, None] for _ in range(3)] for _ in range(4)]
            ahead = mapped(
                lambda p: jnp.where(y < NY - 1, turn_lanes(p, -1), turn_lanes(p, NY - 1)),
                projected(3, -1.0, load),
            )
            hop(3, -1.0, ahead, link_loader(links_ref, 0, low), total)
            behind = mapped(
                lambda p: jnp.where(y > 0, turn_lanes(p, 1), turn_lanes(p, 1 - NY)),
                projected(3, 1.0, load),
            )
            hop(3, 1.0, behind, link_loader(links_ref, 1, low), total)
            at_wall = first_time + 2 * half + row_index(HALF) // BLOCK == when
            for chirality in range(2):
                values = [(load(0, 6 * chirality + i), load(1, 6 * chirality + i)) for i in range(6)]
                for i in range(6):
                    re = MASS * values[i][0]
                    im = MASS * values[i][1]
                    for j in range(6):
                        cre = clover_ref[chirality, 0, i, j].astype(F32)[low : low + HALF]
                        cim = clover_ref[chirality, 1, i, j].astype(F32)[low : low + HALF]
                        re = re + (cre * values[j][0] - cim * values[j][1])
                        im = im + (cre * values[j][1] + cim * values[j][0])
                    s = 2 * chirality + i // 3
                    colour = i % 3
                    here = spin == s
                    sre = jnp.where(here, wall_ref[colour, 0, r], 0.0)
                    sim = jnp.where(here, wall_ref[colour, 1, r], 0.0)
                    re = jnp.where(at_wall, sre, 0.0) + (0.5 * total[s][colour][0] - re)
                    im = jnp.where(at_wall, sim, 0.0) + (0.5 * total[s][colour][1] - im)
                    out_ref[r, 6 * chirality + i, low : low + HALF, :] = re
                    out_ref[r, 12 + 6 * chirality + i, low : low + HALF, :] = im
        return carry

    lax.fori_loop(0, 4, rhs, 0)

    def spread(index, carry):
        start = pl.multiple_of(24 * index, 24)
        block = stencil_ref[pl.ds(start, 24)].reshape((24 * HALF, 24))
        block = jnp.concatenate([block, jnp.zeros((24 * HALF, LANES - 24), F32)], axis=1)
        block = block + turn_lanes(block, 32)
        block = block + turn_lanes(block, 64)
        operator_ref[pl.ds(start, 24)] = block.reshape((24, HALF, LANES))
        return carry

    lax.fori_loop(0, 18, spread, 0, unroll=3)


def centre(wide, wall_time, spin_index, wall, links, clover, stencil):
    vm = pl.BlockSpec(memory_space=pltpu.VMEM)
    hbm = pl.BlockSpec(memory_space=pltpu.HBM)
    return pl.pallas_call(
        centre_kernel,
        out_shape=(
            jax.ShapeDtypeStruct((4, 24, ROWS, LANES), F32),
            jax.ShapeDtypeStruct((9 * 2 * 24, HALF, LANES), F32),
        ),
        in_specs=[vm] + [hbm] * 6,
        out_specs=(vm, vm),
        scratch_shapes=[
            pltpu.VMEM((2, 2, 3, 3, ROWS, LANES), BF16),
            pltpu.VMEM((2, 2, 6, 6, ROWS, LANES), BF16),
            pltpu.VMEM((9 * 2 * 24, HALF, 24), F32),
            pltpu.SMEM((4,), jnp.int32),
            pltpu.SMEM((4,), jnp.int32),
            pltpu.SMEM((3, 2, 4), F32),
            pltpu.SemaphoreType.DMA((6,)),
        ],
        compiler_params=vmem_params(54),
        cost_estimate=pl.CostEstimate(flops=40_000_000, bytes_accessed=20_000_000, transcendentals=0),
    )(wide, wall_time, spin_index, wall, links, clover, stencil)


def fine_kernel(
    wide_ref, partial_ref, tb_ref, zb_ref, xb_ref, ta_ref, za_ref, xa_ref, links_ref, near_ref,
    out_ref, tedge, zedge, xedge, residual, rows_ref,
):
    even = [is_even(axis) for axis in ("ta", "gz", "xy")]
    slabs = ((ta_ref, tb_ref), (za_ref, zb_ref), (xa_ref, xb_ref))
    for direction in range(3):
        for side, sign in enumerate((-1.0, 1.0)):
            toward_a, toward_b = slabs[direction]

            def load(part, component):
                a = toward_a[12 * part + component].astype(F32)
                b = toward_b[12 * part + component].astype(F32)
                return jnp.where(even[direction], a, b) if side == 0 else jnp.where(even[direction], b, a)

            edge = projected(direction, sign, load)
            for s in range(2):
                for colour in range(3):
                    for part in range(2):
                        slot = 6 * s + 2 * colour + part
                        value = edge[s][colour][part]
                        if direction == 0:
                            for r in range(4):
                                tedge[side, slot, r, 0:4, :] = value[4 * r : 4 * r + 4]
                                tedge[side, slot, r, 4:8, :] = value[4 * r : 4 * r + 4]
                        elif direction == 1:
                            zedge[side, slot] = value
                        else:
                            xedge[side, slot] = value
    lanes = lane_index(HALF)
    sub = row_index(HALF)
    upper = sub >= 4
    z = sub % BLOCK

    def rhs(r, carry):
        def table(read):
            return [[tuple(read(6 * s + 2 * colour + part) for part in range(2)) for colour in range(3)] for s in range(2)]

        for half in range(2):
            low = HALF * half

            def loader(start):
                def load(part, component):
                    return wide_ref[part, r, component, start : start + HALF, :]
                return load

            total = [[[None, None] for _ in range(3)] for _ in range(4)]
            for side, sign in enumerate((-1.0, 1.0)):
                def turned(start):
                    return mapped(lambda p: pltpu.roll(p, 4, 0), projected(0, sign, loader(start)))

                edge = table(lambda slot: tedge[side, slot, r])
                if side == 0:
                    lower_part, upper_part = (turned(0), turned(8)) if half == 0 else (turned(8), edge)
                else:
                    lower_part, upper_part = (edge, turned(0)) if half == 0 else (turned(0), turned(8))
                field = mapped(lambda a, b: jnp.where(upper, b, a), lower_part, upper_part)
                hop(0, sign, field, link_loader(links_ref, side, low), total)
            for side, sign in enumerate((-1.0, 1.0)):
                row = 4 * r + 2 * half
                first = table(lambda slot: zedge[side, slot, pl.ds(row, 1), :])
                second = table(lambda slot: zedge[side, slot, pl.ds(row + 1, 1), :])
                shift, place = (HALF - 1, 3) if side == 0 else (1, 0)
                field = mapped(
                    lambda p, a, b: jnp.where(z == place, jnp.where(upper, b, a), pltpu.roll(p, shift, 0)),
                    projected(1, sign, loader(low)), first, second,
                )
                hop(1, sign, field, link_loader(links_ref, 2 + side, low), total)
            for side, sign in enumerate((-1.0, 1.0)):
                edge = table(lambda slot: xedge[side, slot, low : low + HALF, :])
                if side == 0:
                    inside = lanes < 96
                    amount = lax.rem(96 - 32 * r + LANES, LANES)
                    shift = LANES - 32
                else:
                    inside = lanes >= 32
                    amount = lax.rem(LANES - 32 * r, LANES)
                    shift = 32
                field = mapped(
                    lambda p, e: jnp.where(inside, pltpu.roll(p, shift, 1), pltpu.roll(e, amount, 1)),
                    projected(2, sign, loader(low)), edge,
                )
                hop(2, sign, field, link_loader(links_ref, 4 + side, low), total)
            for s in range(4):
                for colour in range(3):
                    for part in range(2):
                        position = 12 * part + 3 * s + colour
                        residual[r, position, low : low + HALF, :] = (
                            partial_ref[r, position, low : low + HALF, :] + 0.5 * total[s][colour][part]
                        )
        return carry

    lax.fori_loop(0, 4, rhs, 0)

    for part in range(2):
        rows_ref[part] = jnp.zeros((LANES, LANES), F32)

    def vector(v, carry):
        for chirality in range(2):
            acc = [[None, None] for _ in range(4)]
            for c in range(6):
                position = 6 * chirality + c
                nre16 = near_ref[v, 0, position].astype(F32)
                nim16 = near_ref[v, 1, position].astype(F32)
                for half in range(2):
                    low = HALF * half
                    nre = nre16[low : low + HALF]
                    nim = nim16[low : low + HALF]
                    for r in range(4):
                        rre = residual[r, position, low : low + HALF, :]
                        rim = residual[r, 12 + position, low : low + HALF, :]
                        tre = nre * rre + nim * rim
                        tim = nre * rim - nim * rre
                        acc[r][0] = tre if acc[r][0] is None else acc[r][0] + tre
                        acc[r][1] = tim if acc[r][1] is None else acc[r][1] + tim
            for r in range(4):
                for part in range(2):
                    rows_ref[part, pl.ds(r * 32 + chirality * 12 + v, 1), :] = jnp.sum(
                        acc[r][part], axis=0, keepdims=True
                    )
        return carry

    lax.fori_loop(0, 12, vector, 0)
    member = ((lane_index(HALF) % NY) // BLOCK == row_index(HALF)).astype(F32)
    for part in range(2):
        out_ref[part] = lax.dot_general(
            member, rows_ref[part], (((1,), (1,)), ((), ())),
            precision=lax.Precision.HIGHEST, preferred_element_type=F32,
        )


def fine(wide, partial, halos, links, near):
    vm = pl.BlockSpec(memory_space=pltpu.VMEM)
    return pl.pallas_call(
        fine_kernel,
        out_shape=jax.ShapeDtypeStruct((2, HALF, LANES), F32),
        in_specs=[vm] * 10,
        out_specs=vm,
        scratch_shapes=[
            pltpu.VMEM((2, 12, 4, HALF, LANES), F32),
            pltpu.VMEM((2, 12, ROWS, LANES), F32),
            pltpu.VMEM((2, 12, ROWS, LANES), F32),
            pltpu.VMEM((4, 24, ROWS, LANES), F32),
            pltpu.VMEM((2, LANES, LANES), F32),
        ],
        compiler_params=vmem_params(24),
        cost_estimate=pl.CostEstimate(flops=40_000_000, bytes_accessed=20_000_000, transcendentals=0),
    )(wide, partial, *[halos[i] for i in (1, 3, 5, 0, 2, 4)], links, near)


def merge(low, high, width, inside):
    if high is None:
        high = jnp.zeros_like(low)
    keep = jnp.where(inside, low, high)
    other = jnp.where(inside, high, low)
    return keep + jnp.where(inside, turn_lanes(other, -width), turn_lanes(other, width))


def coarse_step(estimate, neighbours, restricted_ref, operator_ref):
    members = [estimate] + neighbours
    lanes = lane_index(HALF)
    out = []
    sums = [[None] * 24, [None] * 24]
    for i in range(24):
        re = None
        im = None
        for k in range(9):
            cre = operator_ref[(k * 2) * 24 + i]
            cim = operator_ref[(k * 2 + 1) * 24 + i]
            ere, eim = members[k]
            tre = cre * ere - cim * eim
            tim = cre * eim + cim * ere
            re = tre if re is None else re + tre
            im = tim if im is None else im + tim
        sums[0][i] = re
        sums[1][i] = im
    for part in range(2):
        values = sums[part] + [None] * 8
        width = 16
        while width >= 1:
            inside = (lanes // width) % 2 == 0
            count = width
            values = [
                None if values[i] is None else merge(values[i], values[i + count], width, inside)
                for i in range(count)
            ]
            width //= 2
        out.append(restricted_ref[part] + values[0])
    return out


def coarse_neighbours(estimate, refs):
    neighbours = []
    for direction, axis in enumerate(("ta", "gz", "xy")):
        even = is_even(axis)
        a = refs[2 * direction]
        b = refs[2 * direction + 1]
        neighbours.append(tuple(jnp.where(even, a[part], b[part]) for part in range(2)))
        neighbours.append(tuple(jnp.where(even, b[part], a[part]) for part in range(2)))
    neighbours.append(tuple(pltpu.roll(value, HALF - 1, 0) for value in estimate))
    neighbours.append(tuple(pltpu.roll(value, 1, 0) for value in estimate))
    return neighbours


def coarse_kernel(e_ref, xa, za, ta, xb, zb, tb, r_ref, operator_ref, out_ref):
    estimate = (e_ref[0], e_ref[1])
    out = coarse_step(estimate, coarse_neighbours(estimate, (ta, tb, za, zb, xa, xb)), r_ref, operator_ref)
    out_ref[0] = out[0]
    out_ref[1] = out[1]


def coarse(estimate, halos, restricted, operator):
    vm = pl.BlockSpec(memory_space=pltpu.VMEM)
    return pl.pallas_call(
        coarse_kernel,
        out_shape=jax.ShapeDtypeStruct((2, HALF, LANES), F32),
        in_specs=[vm] * 9,
        out_specs=vm,
        compiler_params=vmem_params(16),
    )(estimate, *[halos[i] for i in (4, 2, 0, 5, 3, 1)], restricted, operator)


def last_kernel(e_ref, xa, za, ta, xb, zb, tb, r_ref, operator_ref, psi_ref, near_ref, out_hbm, out_ref, wide, sems):
    estimate = (e_ref[0], e_ref[1])
    final = coarse_step(estimate, coarse_neighbours(estimate, (ta, tb, za, zb, xa, xb)), r_ref, operator_ref)
    member = ((lane_index(HALF) % NY) // BLOCK == row_index(HALF)).astype(F32)
    for part in range(2):
        wide[part] = lax.dot_general(
            final[part], member, (((0,), (0,)), ((), ())),
            precision=lax.Precision.HIGHEST, preferred_element_type=F32,
        )

    def component(c, carry):
        base = (c // 6) * 12
        near = [(near_ref[v, 0, c].astype(F32), near_ref[v, 1, c].astype(F32)) for v in range(12)]
        for r in range(4):
            re = psi_ref[0, r, c]
            im = psi_ref[1, r, c]
            for v in range(12):
                ere = wide[0, pl.ds(r * 32 + base + v, 1), :]
                eim = wide[1, pl.ds(r * 32 + base + v, 1), :]
                nre, nim = near[v]
                re = re + (nre * ere - nim * eim)
                im = im + (nre * eim + nim * ere)
            out_ref[c, 0, r] = re
            out_ref[c, 1, r] = im
        for part in range(2):
            pltpu.make_async_copy(out_ref.at[c, part], out_hbm.at[part, :, c], sems.at[c, part]).start()
        return carry

    lax.fori_loop(0, 12, component, 0)
    for c in range(12):
        for part in range(2):
            pltpu.make_async_copy(out_ref.at[c, part], out_hbm.at[part, :, c], sems.at[c, part]).wait()


def last(estimate, halos, restricted, operator, psi, near):
    vm = pl.BlockSpec(memory_space=pltpu.VMEM)
    return pl.pallas_call(
        last_kernel,
        out_shape=jax.ShapeDtypeStruct((2, 4, 12, ROWS, LANES), F32),
        in_specs=[vm] * 11,
        out_specs=pl.BlockSpec(memory_space=pltpu.HBM),
        scratch_shapes=[
            pltpu.VMEM((12, 2, 4, ROWS, LANES), F32),
            pltpu.VMEM((2, LANES, LANES), F32),
            pltpu.SemaphoreType.DMA((12, 2)),
        ],
        compiler_params=vmem_params(24),
    )(estimate, *[halos[i] for i in (4, 2, 0, 5, 3, 1)], restricted, operator, psi, near)


def exchange(values):
    halos = [None] * 6
    for which in (4, 2, 0, 5, 3, 1):
        halos[which] = swap(values[which], ("ta", "gz", "xy")[which // 2], which % 2)
    return halos


def local(
    fine_solution, links, clover, near_null, coarse_links, wall_time, spin_index, wall_colour
):
    psi = fine_solution.reshape((2, 4, 12, ROWS, LANES))
    links = links.reshape((8, 2, 3, 3, ROWS, LANES))
    clover = clover.reshape((2, 2, 6, 6, ROWS, LANES))
    near = near_null.reshape((12, 2, 12, ROWS, LANES))
    stencil = jnp.transpose(coarse_links, (0, 1, 2, 4, 5, 6, 3)).reshape((9 * 2 * 24, HALF, 24))
    wall = jnp.transpose(wall_colour, (2, 0, 1))
    *slabs, wide = pack(psi)
    halos = exchange(slabs)
    partial, operator = centre(wide, wall_time, spin_index, wall, links, clover, stencil)
    restricted = fine(wide, partial, halos, links, near)
    estimate = restricted
    for step in range(ITERS - 1):
        estimate = coarse(estimate, exchange([estimate] * 6), restricted, operator)
    result = last(estimate, exchange([estimate] * 6), restricted, operator, wide, near)
    return result.reshape(fine_solution.shape)


def solution(mesh):
    placed = (
        P(None, None, None, "ta", "gz", "xy"),
        P(None, None, None, None, "ta", "gz", "xy"),
        P(None, None, None, None, "ta", "gz", "xy"),
        P(None, None, None, "ta", "gz", "xy"),
        P(None, None, None, None, "ta", "gz", "xy"),
        P(),
        P(),
        P(),
    )
    return jax.shard_map(
        local,
        mesh=mesh,
        in_specs=placed,
        out_specs=P(None, None, None, "ta", "gz", "xy"),
        check_vma=False,
    )
```

```python
import jax
import jax.numpy as jnp
from jax import lax
from jax.experimental import pallas as pl
from jax.experimental.pallas import tpu as pltpu
from jax.sharding import PartitionSpec as P

BLOCK = 4
ITERS = 4
NY = 32
ROWS = 16
LANES = 128
HALF = 8
MASS = 4.1
F32 = jnp.float32
BF16 = jnp.bfloat16

gammas = [
    [[0j, 0j, 1 + 0j, 0j], [0j, 0j, 0j, 1 + 0j], [1 + 0j, 0j, 0j, 0j], [0j, 1 + 0j, 0j, 0j]],
    [[0j, 0j, 1j, 0j], [0j, 0j, 0j, -1j], [-1j, 0j, 0j, 0j], [0j, 1j, 0j, 0j]],
    [[0j, 0j, 0j, 1j], [0j, 0j, 1j, 0j], [0j, -1j, 0j, 0j], [-1j, 0j, 0j, 0j]],
    [[0j, 0j, 0j, -1 + 0j], [0j, 0j, 1 + 0j, 0j], [0j, 1 + 0j, 0j, 0j], [-1 + 0j, 0j, 0j, 0j]],
]


def vmem_params(mib):
    return pltpu.CompilerParams(vmem_limit_bytes=mib * 1024 * 1024)


def lane_index(rows):
    return lax.broadcasted_iota(jnp.int32, (rows, LANES), 1)


def row_index(rows):
    return lax.broadcasted_iota(jnp.int32, (rows, LANES), 0)


def turn_lanes(value, shift):
    return pltpu.roll(value, shift % LANES, 1)


def swap(value, axis, matching):
    count = lax.axis_size(axis)
    if matching == 0:
        pairs = [(i, i ^ 1) for i in range(count)]
    else:
        pairs = [(i, (i + 1 if i % 2 else i - 1) % count) for i in range(count)]
    return lax.ppermute(value, axis, pairs)


def is_even(axis):
    return lax.rem(lax.axis_index(axis), 2) == 0


def pack_kernel(psi_ref, ta_ref, tb_ref, za_ref, zb_ref, xa_ref, xb_ref, wide_ref):
    lanes = lane_index(ROWS)
    even = [is_even(axis) for axis in ("ta", "gz", "xy")]

    def store(component, which, first, last):
        toward_a, toward_b = ((ta_ref, tb_ref), (za_ref, zb_ref), (xa_ref, xb_ref))[which]
        toward_a[component] = jnp.where(even[which], last, first).astype(BF16)
        toward_b[component] = jnp.where(even[which], first, last).astype(BF16)

    def body(component, carry):
        part = component // 12
        c = component % 12
        fields = [psi_ref[part, r, c].astype(F32) for r in range(4)]
        for r in range(4):
            wide_ref[part, r, c] = fields[r]
        store(
            component, 0,
            jnp.concatenate([wide_ref[part, r, c, 0:4, :] for r in range(4)], axis=0),
            jnp.concatenate([wide_ref[part, r, c, 12:16, :] for r in range(4)], axis=0),
        )
        store(
            component, 1,
            jnp.concatenate([wide_ref[part, r, c, pl.ds(0, 4, stride=4), :] for r in range(4)], axis=0),
            jnp.concatenate([wide_ref[part, r, c, pl.ds(3, 4, stride=4), :] for r in range(4)], axis=0),
        )
        low = fields[0]
        high = turn_lanes(fields[0], 32)
        for r in range(1, 4):
            mask = lanes >= 32 * r
            low = jnp.where(mask, turn_lanes(fields[r], 32 * r), low)
            high = jnp.where(mask, turn_lanes(fields[r], 32 * r + 32), high)
        store(component, 2, low, high)
        return carry

    lax.fori_loop(0, 24, body, 0, unroll=4)


def pack(psi):
    slab = jax.ShapeDtypeStruct((24, ROWS, LANES), BF16)
    wide = jax.ShapeDtypeStruct((2, 4, 12, ROWS, LANES), F32)
    vm = pl.BlockSpec(memory_space=pltpu.VMEM)
    return pl.pallas_call(
        pack_kernel,
        out_shape=(slab,) * 6 + (wide,),
        in_specs=[vm],
        out_specs=(vm,) * 7,
        compiler_params=vmem_params(16),
        cost_estimate=pl.CostEstimate(flops=40_000_000, bytes_accessed=40_000_000, transcendentals=0),
    )(psi)


def times(entry, re, im):
    if entry.real != 0:
        return (entry.real, re), (entry.real, im)
    return (-entry.imag, im), (entry.imag, re)


def add_signed(total, term):
    sign, value = term
    if total is None:
        return value if sign > 0 else -value
    return total + value if sign > 0 else total - value


def projected(direction, sign, load):
    rows = []
    for s in range(2):
        partner = 2 if gammas[direction][s][2] != 0 else 3
        entry = gammas[direction][s][partner] * sign
        row = []
        for colour in range(3):
            a, b = times(entry, load(0, 3 * partner + colour), load(1, 3 * partner + colour))
            row.append((
                add_signed(load(0, 3 * s + colour), a),
                add_signed(load(1, 3 * s + colour), b),
            ))
        rows.append(row)
    return rows


def mapped(function, *tables):
    return [
        [
            tuple(function(*[table[s][colour][part] for table in tables]) for part in range(2))
            for colour in range(3)
        ]
        for s in range(2)
    ]


def hop(direction, sign, half_field, link, total):
    for out in range(3):
        row = [link(0, out, inn) for inn in range(3)], [link(1, out, inn) for inn in range(3)]
        moved = []
        for s in range(2):
            re = None
            im = None
            for inn in range(3):
                ure, uim = row[0][inn], row[1][inn]
                hre, him = half_field[s][inn]
                tre = ure * hre - uim * him
                tim = ure * him + uim * hre
                re = tre if re is None else re + tre
                im = tim if im is None else im + tim
            moved.append((re, im))
        for s in range(2):
            for part in range(2):
                total[s][out][part] = add_signed(total[s][out][part], (1.0, moved[s][part]))
        for s in range(2, 4):
            source = 0 if gammas[direction][s][0] != 0 else 1
            entry = gammas[direction][s][source] * sign
            terms = times(entry, *moved[source])
            for part in range(2):
                total[s][out][part] = add_signed(total[s][out][part], terms[part])


def link_loader(links_ref, number, low):
    def link(part, out, inn):
        return links_ref[number, part, out, inn].astype(F32)[low : low + HALF]
    return link


def sideways_kernel(wide_ref, out_ref):
    y = lane_index(HALF) % NY

    def rhs(r, carry):
        for half in range(2):
            low = HALF * half

            def load(part, component):
                return wide_ref[part, r, component, low : low + HALF, :]

            ahead = mapped(
                lambda p: jnp.where(y < NY - 1, turn_lanes(p, -1), turn_lanes(p, NY - 1)),
                projected(3, -1.0, load),
            )
            behind = mapped(
                lambda p: jnp.where(y > 0, turn_lanes(p, 1), turn_lanes(p, 1 - NY)),
                projected(3, 1.0, load),
            )
            for side, field in enumerate((ahead, behind)):
                for s in range(2):
                    for colour in range(3):
                        for part in range(2):
                            out_ref[side, r, 6 * s + 2 * colour + part, low : low + HALF, :] = field[s][colour][part]
        return carry

    lax.fori_loop(0, 4, rhs, 0)


def sideways(wide):
    vm = pl.BlockSpec(memory_space=pltpu.VMEM)
    return pl.pallas_call(
        sideways_kernel,
        out_shape=jax.ShapeDtypeStruct((2, 4, 12, ROWS, LANES), F32),
        in_specs=[vm],
        out_specs=vm,
        compiler_params=vmem_params(8),
        cost_estimate=pl.CostEstimate(flops=40_000_000, bytes_accessed=20_000_000, transcendentals=0),
    )(wide)


def centre_kernel(
    wide_ref, side_ref, when_ref, spin_ref, wall_ref, links_ref, clover_ref, out_ref,
):
    first_time = lax.axis_index("ta") * BLOCK

    def rhs(r, carry):
        when = when_ref[r]
        spin = spin_ref[r]
        for half in range(2):
            low = HALF * half

            def load(part, component):
                return wide_ref[part, r, component, low : low + HALF, :]

            total = [[[None, None] for _ in range(3)] for _ in range(4)]
            for side, sign in enumerate((-1.0, 1.0)):
                field = [
                    [
                        tuple(side_ref[side, r, 6 * s + 2 * colour + part, low : low + HALF, :] for part in range(2))
                        for colour in range(3)
                    ]
                    for s in range(2)
                ]
                hop(3, sign, field, link_loader(links_ref, 6 + side, low), total)
            at_wall = first_time + 2 * half + row_index(HALF) // BLOCK == when
            for chirality in range(2):
                values = [(load(0, 6 * chirality + i), load(1, 6 * chirality + i)) for i in range(6)]
                for i in range(6):
                    re = MASS * values[i][0]
                    im = MASS * values[i][1]
                    for j in range(6):
                        cre = clover_ref[chirality, 0, i, j].astype(F32)[low : low + HALF]
                        cim = clover_ref[chirality, 1, i, j].astype(F32)[low : low + HALF]
                        re = re + (cre * values[j][0] - cim * values[j][1])
                        im = im + (cre * values[j][1] + cim * values[j][0])
                    s = 2 * chirality + i // 3
                    colour = i % 3
                    here = spin == s
                    sre = jnp.where(here, wall_ref[colour, 0, r], 0.0)
                    sim = jnp.where(here, wall_ref[colour, 1, r], 0.0)
                    re = jnp.where(at_wall, sre, 0.0) + (0.5 * total[s][colour][0] - re)
                    im = jnp.where(at_wall, sim, 0.0) + (0.5 * total[s][colour][1] - im)
                    out_ref[r, 6 * chirality + i, low : low + HALF, :] = re
                    out_ref[r, 12 + 6 * chirality + i, low : low + HALF, :] = im
        return carry

    lax.fori_loop(0, 4, rhs, 0)


def centre(wide, side, wall_time, spin_index, wall, links, clover):
    vm = pl.BlockSpec(memory_space=pltpu.VMEM)
    sm = pl.BlockSpec(memory_space=pltpu.SMEM)
    return pl.pallas_call(
        centre_kernel,
        out_shape=jax.ShapeDtypeStruct((4, 24, ROWS, LANES), F32),
        in_specs=[vm] * 2 + [sm] * 3 + [vm] * 2,
        out_specs=vm,
        compiler_params=vmem_params(16),
        cost_estimate=pl.CostEstimate(flops=40_000_000, bytes_accessed=20_000_000, transcendentals=0),
    )(wide, side, wall_time, spin_index, wall, links, clover)


def spread_kernel(stencil_ref, operator_ref):
    def body(k, carry):
        parts = []
        for part in range(2):
            start = pl.multiple_of(48 * k + 24 * part, 24)
            block = stencil_ref[pl.ds(start, 24)].reshape((24 * HALF, 24))
            block = jnp.concatenate([block, jnp.zeros((24 * HALF, LANES - 24), F32)], axis=1)
            block = block + turn_lanes(block, 32)
            parts.append(block + turn_lanes(block, 64))
        operator_ref[k, 0] = parts[0].reshape((24, HALF, LANES))
        operator_ref[k, 1] = parts[1].reshape((24, HALF, LANES))
        operator_ref[k, 2] = (parts[0] + parts[1]).reshape((24, HALF, LANES))
        return carry

    lax.fori_loop(0, 9, body, 0)


def spread(stencil):
    vm = pl.BlockSpec(memory_space=pltpu.VMEM)
    return pl.pallas_call(
        spread_kernel,
        out_shape=jax.ShapeDtypeStruct((9, 3, 24, HALF, LANES), F32),
        in_specs=[vm],
        out_specs=vm,
        compiler_params=vmem_params(8),
    )(stencil)


def fine_kernel(
    wide_ref, partial_ref, tb_ref, zb_ref, xb_ref, ta_ref, za_ref, xa_ref, links_ref, near_ref,
    out_ref, tedge, zedge, xedge, residual, rows_ref,
):
    even = [is_even(axis) for axis in ("ta", "gz", "xy")]
    slabs = ((ta_ref, tb_ref), (za_ref, zb_ref), (xa_ref, xb_ref))
    for direction in range(3):
        for side, sign in enumerate((-1.0, 1.0)):
            toward_a, toward_b = slabs[direction]

            def load(part, component):
                a = toward_a[12 * part + component].astype(F32)
                b = toward_b[12 * part + component].astype(F32)
                return jnp.where(even[direction], a, b) if side == 0 else jnp.where(even[direction], b, a)

            edge = projected(direction, sign, load)
            for s in range(2):
                for colour in range(3):
                    for part in range(2):
                        slot = 6 * s + 2 * colour + part
                        value = edge[s][colour][part]
                        if direction == 0:
                            for r in range(4):
                                tedge[side, slot, r, 0:4, :] = value[4 * r : 4 * r + 4]
                                tedge[side, slot, r, 4:8, :] = value[4 * r : 4 * r + 4]
                        elif direction == 1:
                            zedge[side, slot] = value
                        else:
                            xedge[side, slot] = value
    lanes = lane_index(HALF)
    sub = row_index(HALF)
    upper = sub >= 4
    z = sub % BLOCK

    def rhs(r, carry):
        def table(read):
            return [[tuple(read(6 * s + 2 * colour + part) for part in range(2)) for colour in range(3)] for s in range(2)]

        for half in range(2):
            low = HALF * half

            def loader(start):
                def load(part, component):
                    return wide_ref[part, r, component, start : start + HALF, :]
                return load

            total = [[[None, None] for _ in range(3)] for _ in range(4)]
            for side, sign in enumerate((-1.0, 1.0)):
                def turned(start):
                    return mapped(lambda p: pltpu.roll(p, 4, 0), projected(0, sign, loader(start)))

                edge = table(lambda slot: tedge[side, slot, r])
                if side == 0:
                    lower_part, upper_part = (turned(0), turned(8)) if half == 0 else (turned(8), edge)
                else:
                    lower_part, upper_part = (edge, turned(0)) if half == 0 else (turned(0), turned(8))
                field = mapped(lambda a, b: jnp.where(upper, b, a), lower_part, upper_part)
                hop(0, sign, field, link_loader(links_ref, side, low), total)
            for side, sign in enumerate((-1.0, 1.0)):
                row = 4 * r + 2 * half
                first = table(lambda slot: zedge[side, slot, pl.ds(row, 1), :])
                second = table(lambda slot: zedge[side, slot, pl.ds(row + 1, 1), :])
                shift, place = (HALF - 1, 3) if side == 0 else (1, 0)
                field = mapped(
                    lambda p, a, b: jnp.where(z == place, jnp.where(upper, b, a), pltpu.roll(p, shift, 0)),
                    projected(1, sign, loader(low)), first, second,
                )
                hop(1, sign, field, link_loader(links_ref, 2 + side, low), total)
            for side, sign in enumerate((-1.0, 1.0)):
                edge = table(lambda slot: xedge[side, slot, low : low + HALF, :])
                if side == 0:
                    inside = lanes < 96
                    amount = lax.rem(96 - 32 * r + LANES, LANES)
                    shift = LANES - 32
                else:
                    inside = lanes >= 32
                    amount = lax.rem(LANES - 32 * r, LANES)
                    shift = 32
                field = mapped(
                    lambda p, e: jnp.where(inside, pltpu.roll(p, shift, 1), pltpu.roll(e, amount, 1)),
                    projected(2, sign, loader(low)), edge,
                )
                hop(2, sign, field, link_loader(links_ref, 4 + side, low), total)
            for s in range(4):
                for colour in range(3):
                    position = 3 * s + colour
                    re = partial_ref[r, position, low : low + HALF, :] + 0.5 * total[s][colour][0]
                    im = partial_ref[r, 12 + position, low : low + HALF, :] + 0.5 * total[s][colour][1]
                    residual[r, position, low : low + HALF, :] = re
                    residual[r, 12 + position, low : low + HALF, :] = im - re
                    residual[r, 24 + position, low : low + HALF, :] = re + im
        return carry

    lax.fori_loop(0, 4, rhs, 0)

    for part in range(2):
        rows_ref[part] = jnp.zeros((LANES, LANES), F32)

    def vector(v, carry):
        for chirality in range(2):
            acc = [[None] * 3 for _ in range(4)]
            for c in range(6):
                position = 6 * chirality + c
                nre16 = near_ref[v, 0, position].astype(F32)
                nim16 = near_ref[v, 1, position].astype(F32)
                for half in range(2):
                    low = HALF * half
                    nre = nre16[low : low + HALF]
                    nim = nim16[low : low + HALF]
                    factors = (nre - nim, nre, nim)
                    for r in range(4):
                        for form in range(3):
                            term = factors[form] * residual[r, 12 * form + position, low : low + HALF, :]
                            acc[r][form] = term if acc[r][form] is None else acc[r][form] + term
            for r in range(4):
                for part, value in enumerate((acc[r][0] + acc[r][2], acc[r][0] + acc[r][1])):
                    rows_ref[part, pl.ds(r * 32 + chirality * 12 + v, 1), :] = jnp.sum(
                        value, axis=0, keepdims=True
                    )
        return carry

    lax.fori_loop(0, 12, vector, 0)
    member = ((lane_index(HALF) % NY) // BLOCK == row_index(HALF)).astype(F32)
    for part in range(2):
        out_ref[part] = lax.dot_general(
            member, rows_ref[part], (((1,), (1,)), ((), ())),
            precision=lax.Precision.HIGHEST, preferred_element_type=F32,
        )


def fine(wide, partial, halos, links, near):
    vm = pl.BlockSpec(memory_space=pltpu.VMEM)
    return pl.pallas_call(
        fine_kernel,
        out_shape=jax.ShapeDtypeStruct((2, HALF, LANES), F32),
        in_specs=[vm] * 10,
        out_specs=vm,
        scratch_shapes=[
            pltpu.VMEM((2, 12, 4, HALF, LANES), F32),
            pltpu.VMEM((2, 12, ROWS, LANES), F32),
            pltpu.VMEM((2, 12, ROWS, LANES), F32),
            pltpu.VMEM((4, 36, ROWS, LANES), F32),
            pltpu.VMEM((2, LANES, LANES), F32),
        ],
        compiler_params=vmem_params(24),
        cost_estimate=pl.CostEstimate(flops=40_000_000, bytes_accessed=20_000_000, transcendentals=0),
    )(wide, partial, *[halos[i] for i in (1, 3, 5, 0, 2, 4)], links, near)


def merge(low, high, width, inside):
    if high is None:
        high = jnp.zeros_like(low)
    keep = jnp.where(inside, low, high)
    other = jnp.where(inside, high, low)
    return keep + jnp.where(inside, turn_lanes(other, -width), turn_lanes(other, width))


def coarse_step(estimate, neighbours, restricted_ref, operator_ref):
    members = [(re, im - re, re + im) for re, im in [estimate] + neighbours]
    lanes = lane_index(HALF)
    out = []
    sums = [[None] * 24, [None] * 24]
    for i in range(24):
        acc = [None] * 3
        for k in range(9):
            ere, difference, total = members[k]
            terms = (
                operator_ref[k, 2, i] * ere, operator_ref[k, 0, i] * difference, operator_ref[k, 1, i] * total
            )
            for form in range(3):
                acc[form] = terms[form] if acc[form] is None else acc[form] + terms[form]
        sums[0][i] = acc[0] - acc[2]
        sums[1][i] = acc[0] + acc[1]
    for part in range(2):
        values = sums[part] + [None] * 8
        width = 16
        while width >= 1:
            inside = (lanes // width) % 2 == 0
            count = width
            values = [
                None if values[i] is None else merge(values[i], values[i + count], width, inside)
                for i in range(count)
            ]
            width //= 2
        out.append(restricted_ref[part] + values[0])
    return out


def coarse_neighbours(estimate, refs):
    neighbours = []
    for direction, axis in enumerate(("ta", "gz", "xy")):
        even = is_even(axis)
        a = refs[2 * direction]
        b = refs[2 * direction + 1]
        neighbours.append(tuple(jnp.where(even, a[part], b[part]) for part in range(2)))
        neighbours.append(tuple(jnp.where(even, b[part], a[part]) for part in range(2)))
    neighbours.append(tuple(pltpu.roll(value, HALF - 1, 0) for value in estimate))
    neighbours.append(tuple(pltpu.roll(value, 1, 0) for value in estimate))
    return neighbours


def coarse_kernel(e_ref, xa, za, ta, xb, zb, tb, r_ref, operator_ref, out_ref):
    estimate = (e_ref[0], e_ref[1])
    out = coarse_step(estimate, coarse_neighbours(estimate, (ta, tb, za, zb, xa, xb)), r_ref, operator_ref)
    out_ref[0] = out[0]
    out_ref[1] = out[1]


def coarse(estimate, halos, restricted, operator):
    vm = pl.BlockSpec(memory_space=pltpu.VMEM)
    return pl.pallas_call(
        coarse_kernel,
        out_shape=jax.ShapeDtypeStruct((2, HALF, LANES), F32),
        in_specs=[vm] * 9,
        out_specs=vm,
        compiler_params=vmem_params(16),
    )(estimate, *[halos[i] for i in (4, 2, 0, 5, 3, 1)], restricted, operator)


def last_kernel(e_ref, xa, za, ta, xb, zb, tb, r_ref, operator_ref, psi_ref, near_ref, out_hbm, out_ref, wide, sems):
    estimate = (e_ref[0], e_ref[1])
    final = coarse_step(estimate, coarse_neighbours(estimate, (ta, tb, za, zb, xa, xb)), r_ref, operator_ref)
    member = ((lane_index(HALF) % NY) // BLOCK == row_index(HALF)).astype(F32)
    spreads = [
        lax.dot_general(
            final[part], member, (((0,), (0,)), ((), ())),
            precision=lax.Precision.HIGHEST, preferred_element_type=F32,
        )
        for part in range(2)
    ]
    wide[0] = spreads[0]
    wide[1] = spreads[1] - spreads[0]
    wide[2] = spreads[0] + spreads[1]

    def component(c, carry):
        base = (c // 6) * 12
        near = []
        for v in range(12):
            nre = near_ref[v, 0, c].astype(F32)
            nim = near_ref[v, 1, c].astype(F32)
            near.append((nre + nim, nre, nim))
        for r in range(4):
            acc = [None] * 3
            for v in range(12):
                for form in range(3):
                    term = near[v][form] * wide[form, pl.ds(r * 32 + base + v, 1), :]
                    acc[form] = term if acc[form] is None else acc[form] + term
            out_ref[c, 0, r] = psi_ref[0, r, c] + (acc[0] - acc[2])
            out_ref[c, 1, r] = psi_ref[1, r, c] + (acc[0] + acc[1])
        for part in range(2):
            pltpu.make_async_copy(out_ref.at[c, part], out_hbm.at[part, :, c], sems.at[c, part]).start()
        return carry

    lax.fori_loop(0, 12, component, 0)
    for c in range(12):
        for part in range(2):
            pltpu.make_async_copy(out_ref.at[c, part], out_hbm.at[part, :, c], sems.at[c, part]).wait()


def last(estimate, halos, restricted, operator, psi, near):
    vm = pl.BlockSpec(memory_space=pltpu.VMEM)
    return pl.pallas_call(
        last_kernel,
        out_shape=jax.ShapeDtypeStruct((2, 4, 12, ROWS, LANES), F32),
        in_specs=[vm] * 11,
        out_specs=pl.BlockSpec(memory_space=pltpu.HBM),
        scratch_shapes=[
            pltpu.VMEM((12, 2, 4, ROWS, LANES), F32),
            pltpu.VMEM((3, LANES, LANES), F32),
            pltpu.SemaphoreType.DMA((12, 2)),
        ],
        compiler_params=vmem_params(24),
    )(estimate, *[halos[i] for i in (4, 2, 0, 5, 3, 1)], restricted, operator, psi, near)


def exchange(values):
    halos = [None] * 6
    for which in (4, 2, 0, 5, 3, 1):
        halos[which] = swap(values[which], ("ta", "gz", "xy")[which // 2], which % 2)
    return halos


def local(
    fine_solution, links, clover, near_null, coarse_links, wall_time, spin_index, wall_colour
):
    psi = fine_solution.reshape((2, 4, 12, ROWS, LANES))
    links = links.reshape((8, 2, 3, 3, ROWS, LANES))
    clover = clover.reshape((2, 2, 6, 6, ROWS, LANES))
    near = near_null.reshape((12, 2, 12, ROWS, LANES))
    stencil = jnp.transpose(coarse_links, (0, 1, 2, 4, 5, 6, 3)).reshape((9 * 2 * 24, HALF, 24))
    wall = jnp.transpose(wall_colour, (2, 0, 1))
    *slabs, wide = pack(psi)
    halos = exchange(slabs)
    partial = centre(wide, sideways(wide), wall_time, spin_index, wall, links, clover)
    operator = spread(stencil)
    restricted = fine(wide, partial, halos, links, near)
    estimate = restricted
    for step in range(ITERS - 1):
        estimate = coarse(estimate, exchange([estimate] * 6), restricted, operator)
    result = last(estimate, exchange([estimate] * 6), restricted, operator, wide, near)
    return result.reshape(fine_solution.shape)


def solution(mesh):
    placed = (
        P(None, None, None, "ta", "gz", "xy"),
        P(None, None, None, None, "ta", "gz", "xy"),
        P(None, None, None, None, "ta", "gz", "xy"),
        P(None, None, None, "ta", "gz", "xy"),
        P(None, None, None, None, "ta", "gz", "xy"),
        P(),
        P(),
        P(),
    )
    return jax.shard_map(
        local,
        mesh=mesh,
        in_specs=placed,
        out_specs=P(None, None, None, "ta", "gz", "xy"),
        check_vma=False,
    )
```

```python
import jax
import jax.numpy as jnp
from jax import lax
from jax.experimental import pallas as pl
from jax.experimental.pallas import tpu as pltpu
from jax.sharding import PartitionSpec as P

BLOCK = 4
ITERS = 4
NY = 32
ROWS = 16
LANES = 128
HALF = 8
MASS = 4.1
F32 = jnp.float32
BF16 = jnp.bfloat16

gammas = [
    [[0j, 0j, 1 + 0j, 0j], [0j, 0j, 0j, 1 + 0j], [1 + 0j, 0j, 0j, 0j], [0j, 1 + 0j, 0j, 0j]],
    [[0j, 0j, 1j, 0j], [0j, 0j, 0j, -1j], [-1j, 0j, 0j, 0j], [0j, 1j, 0j, 0j]],
    [[0j, 0j, 0j, 1j], [0j, 0j, 1j, 0j], [0j, -1j, 0j, 0j], [-1j, 0j, 0j, 0j]],
    [[0j, 0j, 0j, -1 + 0j], [0j, 0j, 1 + 0j, 0j], [0j, 1 + 0j, 0j, 0j], [-1 + 0j, 0j, 0j, 0j]],
]


def vmem_params(mib):
    return pltpu.CompilerParams(vmem_limit_bytes=mib * 1024 * 1024)


def lane_index(rows):
    return lax.broadcasted_iota(jnp.int32, (rows, LANES), 1)


def row_index(rows):
    return lax.broadcasted_iota(jnp.int32, (rows, LANES), 0)


def turn_lanes(value, shift):
    return pltpu.roll(value, shift % LANES, 1)


def swap(value, axis, matching):
    count = lax.axis_size(axis)
    if matching == 0:
        pairs = [(i, i ^ 1) for i in range(count)]
    else:
        pairs = [(i, (i + 1 if i % 2 else i - 1) % count) for i in range(count)]
    return lax.ppermute(value, axis, pairs)


def is_even(axis):
    return lax.rem(lax.axis_index(axis), 2) == 0


def pack_kernel(psi_ref, ta_ref, tb_ref, za_ref, zb_ref, xa_ref, xb_ref, wide_ref):
    lanes = lane_index(ROWS)
    even = [is_even(axis) for axis in ("ta", "gz", "xy")]

    def store(component, which, first, last):
        toward_a, toward_b = ((ta_ref, tb_ref), (za_ref, zb_ref), (xa_ref, xb_ref))[which]
        toward_a[component] = jnp.where(even[which], last, first).astype(BF16)
        toward_b[component] = jnp.where(even[which], first, last).astype(BF16)

    def body(component, carry):
        part = component // 12
        c = component % 12
        fields = [psi_ref[part, r, c].astype(F32) for r in range(4)]
        for r in range(4):
            wide_ref[part, r, c] = fields[r]
        store(
            component, 0,
            jnp.concatenate([wide_ref[part, r, c, 0:4, :] for r in range(4)], axis=0),
            jnp.concatenate([wide_ref[part, r, c, 12:16, :] for r in range(4)], axis=0),
        )
        store(
            component, 1,
            jnp.concatenate([wide_ref[part, r, c, pl.ds(0, 4, stride=4), :] for r in range(4)], axis=0),
            jnp.concatenate([wide_ref[part, r, c, pl.ds(3, 4, stride=4), :] for r in range(4)], axis=0),
        )
        low = fields[0]
        high = turn_lanes(fields[0], 32)
        for r in range(1, 4):
            mask = lanes >= 32 * r
            low = jnp.where(mask, turn_lanes(fields[r], 32 * r), low)
            high = jnp.where(mask, turn_lanes(fields[r], 32 * r + 32), high)
        store(component, 2, low, high)
        return carry

    lax.fori_loop(0, 24, body, 0, unroll=4)


def pack(psi):
    slab = jax.ShapeDtypeStruct((24, ROWS, LANES), BF16)
    wide = jax.ShapeDtypeStruct((2, 4, 12, ROWS, LANES), F32)
    vm = pl.BlockSpec(memory_space=pltpu.VMEM)
    return pl.pallas_call(
        pack_kernel,
        out_shape=(slab,) * 6 + (wide,),
        in_specs=[vm],
        out_specs=(vm,) * 7,
        compiler_params=vmem_params(16),
        cost_estimate=pl.CostEstimate(flops=40_000_000, bytes_accessed=40_000_000, transcendentals=0),
    )(psi)


def times(entry, re, im):
    if entry.real != 0:
        return (entry.real, re), (entry.real, im)
    return (-entry.imag, im), (entry.imag, re)


def add_signed(total, term):
    sign, value = term
    if total is None:
        return value if sign > 0 else -value
    return total + value if sign > 0 else total - value


def projected(direction, sign, load):
    rows = []
    for s in range(2):
        partner = 2 if gammas[direction][s][2] != 0 else 3
        entry = gammas[direction][s][partner] * sign
        row = []
        for colour in range(3):
            a, b = times(entry, load(0, 3 * partner + colour), load(1, 3 * partner + colour))
            row.append((
                add_signed(load(0, 3 * s + colour), a),
                add_signed(load(1, 3 * s + colour), b),
            ))
        rows.append(row)
    return rows


def mapped(function, *tables):
    return [
        [
            tuple(function(*[table[s][colour][part] for table in tables]) for part in range(2))
            for colour in range(3)
        ]
        for s in range(2)
    ]


def hop(direction, sign, half_field, link, total):
    for out in range(3):
        row = [link(0, out, inn) for inn in range(3)], [link(1, out, inn) for inn in range(3)]
        moved = []
        for s in range(2):
            re = None
            im = None
            for inn in range(3):
                ure, uim = row[0][inn], row[1][inn]
                hre, him = half_field[s][inn]
                tre = ure * hre - uim * him
                tim = ure * him + uim * hre
                re = tre if re is None else re + tre
                im = tim if im is None else im + tim
            moved.append((re, im))
        for s in range(2):
            for part in range(2):
                total[s][out][part] = add_signed(total[s][out][part], (1.0, moved[s][part]))
        for s in range(2, 4):
            source = 0 if gammas[direction][s][0] != 0 else 1
            entry = gammas[direction][s][source] * sign
            terms = times(entry, *moved[source])
            for part in range(2):
                total[s][out][part] = add_signed(total[s][out][part], terms[part])


def link_loader(links_ref, number, low):
    def link(part, out, inn):
        return links_ref[number, part, out, inn].astype(F32)[low : low + HALF]
    return link


def sideways_kernel(wide_ref, out_ref):
    y = lane_index(HALF) % NY

    def rhs(r, carry):
        for half in range(2):
            low = HALF * half

            def load(part, component):
                return wide_ref[part, r, component, low : low + HALF, :]

            ahead = mapped(
                lambda p: jnp.where(y < NY - 1, turn_lanes(p, -1), turn_lanes(p, NY - 1)),
                projected(3, -1.0, load),
            )
            behind = mapped(
                lambda p: jnp.where(y > 0, turn_lanes(p, 1), turn_lanes(p, 1 - NY)),
                projected(3, 1.0, load),
            )
            for side, field in enumerate((ahead, behind)):
                for s in range(2):
                    for colour in range(3):
                        for part in range(2):
                            out_ref[side, r, 6 * s + 2 * colour + part, low : low + HALF, :] = field[s][colour][part]
        return carry

    lax.fori_loop(0, 4, rhs, 0)


def sideways(wide):
    vm = pl.BlockSpec(memory_space=pltpu.VMEM)
    return pl.pallas_call(
        sideways_kernel,
        out_shape=jax.ShapeDtypeStruct((2, 4, 12, ROWS, LANES), F32),
        in_specs=[vm],
        out_specs=vm,
        compiler_params=vmem_params(8),
        cost_estimate=pl.CostEstimate(flops=40_000_000, bytes_accessed=20_000_000, transcendentals=0),
    )(wide)


def centre_kernel(
    wide_ref, side_ref, when_ref, spin_ref, wall_ref, links_ref, clover_ref, out_ref,
):
    first_time = lax.axis_index("ta") * BLOCK
    upper = row_index(HALF) >= 4

    def rhs(r, carry):
        when = when_ref[r]
        spin = spin_ref[r]
        for half in range(2):
            low = HALF * half

            def load(part, component):
                return wide_ref[part, r, component, low : low + HALF, :]

            total = [[[None, None] for _ in range(3)] for _ in range(4)]
            for side, sign in enumerate((-1.0, 1.0)):
                field = [
                    [
                        tuple(side_ref[side, r, 6 * s + 2 * colour + part, low : low + HALF, :] for part in range(2))
                        for colour in range(3)
                    ]
                    for s in range(2)
                ]
                hop(3, sign, field, link_loader(links_ref, 6 + side, low), total)
            sign = -1.0 if half == 0 else 1.0
            turned = [
                mapped(
                    lambda p: pltpu.roll(p, 4, 0),
                    projected(0, sign, lambda part, c, start=start: wide_ref[part, r, c, start : start + HALF, :]),
                )
                for start in (0, HALF)
            ]
            field = mapped(lambda a, b: jnp.where(upper, b, a), *turned)
            hop(0, sign, field, link_loader(links_ref, half, low), total)
            at_wall = first_time + 2 * half + row_index(HALF) // BLOCK == when
            for chirality in range(2):
                values = [(load(0, 6 * chirality + i), load(1, 6 * chirality + i)) for i in range(6)]
                for i in range(6):
                    re = MASS * values[i][0]
                    im = MASS * values[i][1]
                    for j in range(6):
                        cre = clover_ref[chirality, 0, i, j].astype(F32)[low : low + HALF]
                        cim = clover_ref[chirality, 1, i, j].astype(F32)[low : low + HALF]
                        re = re + (cre * values[j][0] - cim * values[j][1])
                        im = im + (cre * values[j][1] + cim * values[j][0])
                    s = 2 * chirality + i // 3
                    colour = i % 3
                    here = spin == s
                    sre = jnp.where(here, wall_ref[colour, 0, r], 0.0)
                    sim = jnp.where(here, wall_ref[colour, 1, r], 0.0)
                    re = jnp.where(at_wall, sre, 0.0) + (0.5 * total[s][colour][0] - re)
                    im = jnp.where(at_wall, sim, 0.0) + (0.5 * total[s][colour][1] - im)
                    out_ref[r, 6 * chirality + i, low : low + HALF, :] = re
                    out_ref[r, 12 + 6 * chirality + i, low : low + HALF, :] = im
        return carry

    lax.fori_loop(0, 4, rhs, 0)


def centre(wide, side, wall_time, spin_index, wall, links, clover):
    vm = pl.BlockSpec(memory_space=pltpu.VMEM)
    sm = pl.BlockSpec(memory_space=pltpu.SMEM)
    return pl.pallas_call(
        centre_kernel,
        out_shape=jax.ShapeDtypeStruct((4, 24, ROWS, LANES), F32),
        in_specs=[vm] * 2 + [sm] * 3 + [vm] * 2,
        out_specs=vm,
        compiler_params=vmem_params(16),
        cost_estimate=pl.CostEstimate(flops=40_000_000, bytes_accessed=20_000_000, transcendentals=0),
    )(wide, side, wall_time, spin_index, wall, links, clover)


def spread_kernel(stencil_ref, operator_ref):
    def body(k, carry):
        parts = []
        for part in range(2):
            start = pl.multiple_of(48 * k + 24 * part, 24)
            block = stencil_ref[pl.ds(start, 24)].reshape((24 * HALF, 24))
            block = jnp.concatenate([block, jnp.zeros((24 * HALF, LANES - 24), F32)], axis=1)
            block = block + turn_lanes(block, 32)
            parts.append(block + turn_lanes(block, 64))
        operator_ref[k, 0] = parts[0].reshape((24, HALF, LANES))
        operator_ref[k, 1] = parts[1].reshape((24, HALF, LANES))
        operator_ref[k, 2] = (parts[0] + parts[1]).reshape((24, HALF, LANES))
        return carry

    lax.fori_loop(0, 9, body, 0)


def spread(stencil):
    vm = pl.BlockSpec(memory_space=pltpu.VMEM)
    return pl.pallas_call(
        spread_kernel,
        out_shape=jax.ShapeDtypeStruct((9, 3, 24, HALF, LANES), F32),
        in_specs=[vm],
        out_specs=vm,
        compiler_params=vmem_params(8),
    )(stencil)


def fine_kernel(
    wide_ref, partial_ref, xb_ref, tb_ref, zb_ref, ta_ref, za_ref, xa_ref, links_ref, near_ref,
    out_ref, tedge, zedge, xedge, residual, rows_ref,
):
    even = [is_even(axis) for axis in ("ta", "gz", "xy")]
    slabs = ((ta_ref, tb_ref), (za_ref, zb_ref), (xa_ref, xb_ref))
    for direction in range(3):
        for side, sign in enumerate((-1.0, 1.0)):
            toward_a, toward_b = slabs[direction]

            def load(part, component):
                a = toward_a[12 * part + component].astype(F32)
                b = toward_b[12 * part + component].astype(F32)
                return jnp.where(even[direction], a, b) if side == 0 else jnp.where(even[direction], b, a)

            edge = projected(direction, sign, load)
            for s in range(2):
                for colour in range(3):
                    for part in range(2):
                        slot = 6 * s + 2 * colour + part
                        value = edge[s][colour][part]
                        if direction == 0:
                            for r in range(4):
                                tedge[side, slot, r, 0:4, :] = value[4 * r : 4 * r + 4]
                                tedge[side, slot, r, 4:8, :] = value[4 * r : 4 * r + 4]
                        elif direction == 1:
                            zedge[side, slot] = value
                        else:
                            xedge[side, slot] = value
    lanes = lane_index(HALF)
    sub = row_index(HALF)
    upper = sub >= 4
    z = sub % BLOCK

    def rhs(r, carry):
        def table(read):
            return [[tuple(read(6 * s + 2 * colour + part) for part in range(2)) for colour in range(3)] for s in range(2)]

        for half in range(2):
            low = HALF * half

            def loader(start):
                def load(part, component):
                    return wide_ref[part, r, component, start : start + HALF, :]
                return load

            total = [[[None, None] for _ in range(3)] for _ in range(4)]
            side = 1 if half == 0 else 0
            sign = 1.0 if half == 0 else -1.0
            turned = mapped(lambda p: pltpu.roll(p, 4, 0), projected(0, sign, loader(low)))
            edge = table(lambda slot: tedge[side, slot, r])
            lower_part, upper_part = (edge, turned) if half == 0 else (turned, edge)
            field = mapped(lambda a, b: jnp.where(upper, b, a), lower_part, upper_part)
            hop(0, sign, field, link_loader(links_ref, side, low), total)
            for side, sign in enumerate((-1.0, 1.0)):
                row = 4 * r + 2 * half
                first = table(lambda slot: zedge[side, slot, pl.ds(row, 1), :])
                second = table(lambda slot: zedge[side, slot, pl.ds(row + 1, 1), :])
                shift, place = (HALF - 1, 3) if side == 0 else (1, 0)
                field = mapped(
                    lambda p, a, b: jnp.where(z == place, jnp.where(upper, b, a), pltpu.roll(p, shift, 0)),
                    projected(1, sign, loader(low)), first, second,
                )
                hop(1, sign, field, link_loader(links_ref, 2 + side, low), total)
            for side, sign in enumerate((-1.0, 1.0)):
                edge = table(lambda slot: xedge[side, slot, low : low + HALF, :])
                if side == 0:
                    inside = lanes < 96
                    amount = lax.rem(96 - 32 * r + LANES, LANES)
                    shift = LANES - 32
                else:
                    inside = lanes >= 32
                    amount = lax.rem(LANES - 32 * r, LANES)
                    shift = 32
                field = mapped(
                    lambda p, e: jnp.where(inside, pltpu.roll(p, shift, 1), pltpu.roll(e, amount, 1)),
                    projected(2, sign, loader(low)), edge,
                )
                hop(2, sign, field, link_loader(links_ref, 4 + side, low), total)
            for s in range(4):
                for colour in range(3):
                    position = 3 * s + colour
                    re = partial_ref[r, position, low : low + HALF, :] + 0.5 * total[s][colour][0]
                    im = partial_ref[r, 12 + position, low : low + HALF, :] + 0.5 * total[s][colour][1]
                    residual[r, position, low : low + HALF, :] = re
                    residual[r, 12 + position, low : low + HALF, :] = im - re
                    residual[r, 24 + position, low : low + HALF, :] = re + im
        return carry

    lax.fori_loop(0, 4, rhs, 0)

    for part in range(2):
        rows_ref[part] = jnp.zeros((LANES, LANES), F32)

    def vector(v, carry):
        for chirality in range(2):
            acc = [[None] * 3 for _ in range(4)]
            for c in range(6):
                position = 6 * chirality + c
                nre16 = near_ref[v, 0, position].astype(F32)
                nim16 = near_ref[v, 1, position].astype(F32)
                for half in range(2):
                    low = HALF * half
                    nre = nre16[low : low + HALF]
                    nim = nim16[low : low + HALF]
                    factors = (nre - nim, nre, nim)
                    for r in range(4):
                        for form in range(3):
                            term = factors[form] * residual[r, 12 * form + position, low : low + HALF, :]
                            acc[r][form] = term if acc[r][form] is None else acc[r][form] + term
            for r in range(4):
                for part, value in enumerate((acc[r][0] + acc[r][2], acc[r][0] + acc[r][1])):
                    rows_ref[part, pl.ds(r * 32 + chirality * 12 + v, 1), :] = jnp.sum(
                        value, axis=0, keepdims=True
                    )
        return carry

    lax.fori_loop(0, 12, vector, 0)
    member = ((lane_index(HALF) % NY) // BLOCK == row_index(HALF)).astype(F32)
    for part in range(2):
        out_ref[part] = lax.dot_general(
            member, rows_ref[part], (((1,), (1,)), ((), ())),
            precision=lax.Precision.HIGHEST, preferred_element_type=F32,
        )


def fine(wide, partial, halos, links, near):
    vm = pl.BlockSpec(memory_space=pltpu.VMEM)
    return pl.pallas_call(
        fine_kernel,
        out_shape=jax.ShapeDtypeStruct((2, HALF, LANES), F32),
        in_specs=[vm] * 10,
        out_specs=vm,
        scratch_shapes=[
            pltpu.VMEM((2, 12, 4, HALF, LANES), F32),
            pltpu.VMEM((2, 12, ROWS, LANES), F32),
            pltpu.VMEM((2, 12, ROWS, LANES), F32),
            pltpu.VMEM((4, 36, ROWS, LANES), F32),
            pltpu.VMEM((2, LANES, LANES), F32),
        ],
        compiler_params=vmem_params(24),
        cost_estimate=pl.CostEstimate(flops=40_000_000, bytes_accessed=20_000_000, transcendentals=0),
    )(wide, partial, *[halos[i] for i in (5, 1, 3, 0, 2, 4)], links, near)


def merge(low, high, width, inside):
    if high is None:
        high = jnp.zeros_like(low)
    keep = jnp.where(inside, low, high)
    other = jnp.where(inside, high, low)
    return keep + jnp.where(inside, turn_lanes(other, -width), turn_lanes(other, width))


def coarse_step(estimate, neighbours, restricted_ref, operator_ref):
    members = [(re, im - re, re + im) for re, im in [estimate] + neighbours]
    lanes = lane_index(HALF)
    out = []
    sums = [[None] * 24, [None] * 24]
    for i in range(24):
        acc = [None] * 3
        for k in range(9):
            ere, difference, total = members[k]
            terms = (
                operator_ref[k, 2, i] * ere, operator_ref[k, 0, i] * difference, operator_ref[k, 1, i] * total
            )
            for form in range(3):
                acc[form] = terms[form] if acc[form] is None else acc[form] + terms[form]
        sums[0][i] = acc[0] - acc[2]
        sums[1][i] = acc[0] + acc[1]
    for part in range(2):
        values = sums[part] + [None] * 8
        width = 16
        while width >= 1:
            inside = (lanes // width) % 2 == 0
            count = width
            values = [
                None if values[i] is None else merge(values[i], values[i + count], width, inside)
                for i in range(count)
            ]
            width //= 2
        out.append(restricted_ref[part] + values[0])
    return out


def coarse_neighbours(estimate, refs):
    neighbours = []
    for direction, axis in enumerate(("ta", "gz", "xy")):
        even = is_even(axis)
        a = refs[2 * direction]
        b = refs[2 * direction + 1]
        neighbours.append(tuple(jnp.where(even, a[part], b[part]) for part in range(2)))
        neighbours.append(tuple(jnp.where(even, b[part], a[part]) for part in range(2)))
    neighbours.append(tuple(pltpu.roll(value, HALF - 1, 0) for value in estimate))
    neighbours.append(tuple(pltpu.roll(value, 1, 0) for value in estimate))
    return neighbours


def coarse_kernel(e_ref, xa, za, ta, xb, zb, tb, r_ref, operator_ref, out_ref):
    estimate = (e_ref[0], e_ref[1])
    out = coarse_step(estimate, coarse_neighbours(estimate, (ta, tb, za, zb, xa, xb)), r_ref, operator_ref)
    out_ref[0] = out[0]
    out_ref[1] = out[1]


def coarse(estimate, halos, restricted, operator):
    vm = pl.BlockSpec(memory_space=pltpu.VMEM)
    return pl.pallas_call(
        coarse_kernel,
        out_shape=jax.ShapeDtypeStruct((2, HALF, LANES), F32),
        in_specs=[vm] * 9,
        out_specs=vm,
        compiler_params=vmem_params(16),
    )(estimate, *[halos[i] for i in (4, 2, 0, 5, 3, 1)], restricted, operator)


def last_kernel(e_ref, xa, za, ta, xb, zb, tb, r_ref, operator_ref, psi_ref, near_ref, out_hbm, out_ref, wide, sems):
    estimate = (e_ref[0], e_ref[1])
    final = coarse_step(estimate, coarse_neighbours(estimate, (ta, tb, za, zb, xa, xb)), r_ref, operator_ref)
    member = ((lane_index(HALF) % NY) // BLOCK == row_index(HALF)).astype(F32)
    spreads = [
        lax.dot_general(
            final[part], member, (((0,), (0,)), ((), ())),
            precision=lax.Precision.HIGHEST, preferred_element_type=F32,
        )
        for part in range(2)
    ]
    wide[0] = spreads[0]
    wide[1] = spreads[1] - spreads[0]
    wide[2] = spreads[0] + spreads[1]

    def component(c, carry):
        base = (c // 6) * 12
        near = []
        for v in range(12):
            nre = near_ref[v, 0, c].astype(F32)
            nim = near_ref[v, 1, c].astype(F32)
            near.append((nre + nim, nre, nim))
        for r in range(4):
            acc = [None] * 3
            for v in range(12):
                for form in range(3):
                    term = near[v][form] * wide[form, pl.ds(r * 32 + base + v, 1), :]
                    acc[form] = term if acc[form] is None else acc[form] + term
            out_ref[c, 0, r] = psi_ref[0, r, c] + (acc[0] - acc[2])
            out_ref[c, 1, r] = psi_ref[1, r, c] + (acc[0] + acc[1])
        for part in range(2):
            pltpu.make_async_copy(out_ref.at[c, part], out_hbm.at[part, :, c], sems.at[c, part]).start()
        return carry

    lax.fori_loop(0, 12, component, 0)
    for c in range(12):
        for part in range(2):
            pltpu.make_async_copy(out_ref.at[c, part], out_hbm.at[part, :, c], sems.at[c, part]).wait()


def last(estimate, halos, restricted, operator, psi, near):
    vm = pl.BlockSpec(memory_space=pltpu.VMEM)
    return pl.pallas_call(
        last_kernel,
        out_shape=jax.ShapeDtypeStruct((2, 4, 12, ROWS, LANES), F32),
        in_specs=[vm] * 11,
        out_specs=pl.BlockSpec(memory_space=pltpu.HBM),
        scratch_shapes=[
            pltpu.VMEM((12, 2, 4, ROWS, LANES), F32),
            pltpu.VMEM((3, LANES, LANES), F32),
            pltpu.SemaphoreType.DMA((12, 2)),
        ],
        compiler_params=vmem_params(24),
    )(estimate, *[halos[i] for i in (4, 2, 0, 5, 3, 1)], restricted, operator, psi, near)


def exchange(values):
    halos = [None] * 6
    for which in (4, 2, 0, 5, 3, 1):
        halos[which] = swap(values[which], ("ta", "gz", "xy")[which // 2], which % 2)
    return halos


def local(
    fine_solution, links, clover, near_null, coarse_links, wall_time, spin_index, wall_colour
):
    psi = fine_solution.reshape((2, 4, 12, ROWS, LANES))
    links = links.reshape((8, 2, 3, 3, ROWS, LANES))
    clover = clover.reshape((2, 2, 6, 6, ROWS, LANES))
    near = near_null.reshape((12, 2, 12, ROWS, LANES))
    stencil = jnp.transpose(coarse_links, (0, 1, 2, 4, 5, 6, 3)).reshape((9 * 2 * 24, HALF, 24))
    wall = jnp.transpose(wall_colour, (2, 0, 1))
    *slabs, wide = pack(psi)
    halos = exchange(slabs)
    partial = centre(wide, sideways(wide), wall_time, spin_index, wall, links, clover)
    operator = spread(stencil)
    restricted = fine(wide, partial, halos, links, near)
    estimate = restricted
    for step in range(ITERS - 1):
        estimate = coarse(estimate, exchange([estimate] * 6), restricted, operator)
    result = last(estimate, exchange([estimate] * 6), restricted, operator, wide, near)
    return result.reshape(fine_solution.shape)


def solution(mesh):
    placed = (
        P(None, None, None, "ta", "gz", "xy"),
        P(None, None, None, None, "ta", "gz", "xy"),
        P(None, None, None, None, "ta", "gz", "xy"),
        P(None, None, None, "ta", "gz", "xy"),
        P(None, None, None, None, "ta", "gz", "xy"),
        P(),
        P(),
        P(),
    )
    return jax.shard_map(
        local,
        mesh=mesh,
        in_specs=placed,
        out_specs=P(None, None, None, "ta", "gz", "xy"),
        check_vma=False,
    )
```

```python
import jax
import jax.numpy as jnp
from jax import lax
from jax.experimental import pallas as pl
from jax.experimental.pallas import tpu as pltpu
from jax.sharding import PartitionSpec as P

BLOCK = 4
ITERS = 4
NY = 32
ROWS = 16
LANES = 128
HALF = 8
MASS = 4.1
F32 = jnp.float32
BF16 = jnp.bfloat16

gammas = [
    [[0j, 0j, 1 + 0j, 0j], [0j, 0j, 0j, 1 + 0j], [1 + 0j, 0j, 0j, 0j], [0j, 1 + 0j, 0j, 0j]],
    [[0j, 0j, 1j, 0j], [0j, 0j, 0j, -1j], [-1j, 0j, 0j, 0j], [0j, 1j, 0j, 0j]],
    [[0j, 0j, 0j, 1j], [0j, 0j, 1j, 0j], [0j, -1j, 0j, 0j], [-1j, 0j, 0j, 0j]],
    [[0j, 0j, 0j, -1 + 0j], [0j, 0j, 1 + 0j, 0j], [0j, 1 + 0j, 0j, 0j], [-1 + 0j, 0j, 0j, 0j]],
]


def vmem_params(mib):
    return pltpu.CompilerParams(vmem_limit_bytes=mib * 1024 * 1024)


def lane_index(rows):
    return lax.broadcasted_iota(jnp.int32, (rows, LANES), 1)


def row_index(rows):
    return lax.broadcasted_iota(jnp.int32, (rows, LANES), 0)


def turn_lanes(value, shift):
    return pltpu.roll(value, shift % LANES, 1)


def swap(value, axis, matching):
    count = lax.axis_size(axis)
    if matching == 0:
        pairs = [(i, i ^ 1) for i in range(count)]
    else:
        pairs = [(i, (i + 1 if i % 2 else i - 1) % count) for i in range(count)]
    return lax.ppermute(value, axis, pairs)


def is_even(axis):
    return lax.rem(lax.axis_index(axis), 2) == 0


def pack_kernel(psi_ref, ta_ref, tb_ref, za_ref, zb_ref, xa_ref, xb_ref, wide_ref):
    lanes = lane_index(ROWS)
    even = [is_even(axis) for axis in ("ta", "gz", "xy")]

    def store(component, which, first, last):
        toward_a, toward_b = ((ta_ref, tb_ref), (za_ref, zb_ref), (xa_ref, xb_ref))[which]
        toward_a[component] = jnp.where(even[which], last, first).astype(BF16)
        toward_b[component] = jnp.where(even[which], first, last).astype(BF16)

    def body(component, carry):
        part = component // 12
        c = component % 12
        fields = [psi_ref[part, r, c].astype(F32) for r in range(4)]
        for r in range(4):
            wide_ref[part, r, c] = fields[r]
        store(
            component, 0,
            jnp.concatenate([wide_ref[part, r, c, 0:4, :] for r in range(4)], axis=0),
            jnp.concatenate([wide_ref[part, r, c, 12:16, :] for r in range(4)], axis=0),
        )
        store(
            component, 1,
            jnp.concatenate([wide_ref[part, r, c, pl.ds(0, 4, stride=4), :] for r in range(4)], axis=0),
            jnp.concatenate([wide_ref[part, r, c, pl.ds(3, 4, stride=4), :] for r in range(4)], axis=0),
        )
        low = fields[0]
        high = turn_lanes(fields[0], 32)
        for r in range(1, 4):
            mask = lanes >= 32 * r
            low = jnp.where(mask, turn_lanes(fields[r], 32 * r), low)
            high = jnp.where(mask, turn_lanes(fields[r], 32 * r + 32), high)
        store(component, 2, low, high)
        return carry

    lax.fori_loop(0, 24, body, 0, unroll=4)


def pack(psi):
    slab = jax.ShapeDtypeStruct((24, ROWS, LANES), BF16)
    wide = jax.ShapeDtypeStruct((2, 4, 12, ROWS, LANES), F32)
    vm = pl.BlockSpec(memory_space=pltpu.VMEM)
    return pl.pallas_call(
        pack_kernel,
        out_shape=(slab,) * 6 + (wide,),
        in_specs=[vm],
        out_specs=(vm,) * 7,
        compiler_params=vmem_params(16),
        cost_estimate=pl.CostEstimate(flops=40_000_000, bytes_accessed=40_000_000, transcendentals=0),
    )(psi)


def times(entry, re, im):
    if entry.real != 0:
        return (entry.real, re), (entry.real, im)
    return (-entry.imag, im), (entry.imag, re)


def add_signed(total, term):
    sign, value = term
    if total is None:
        return value if sign > 0 else -value
    return total + value if sign > 0 else total - value


def projected(direction, sign, load):
    rows = []
    for s in range(2):
        partner = 2 if gammas[direction][s][2] != 0 else 3
        entry = gammas[direction][s][partner] * sign
        row = []
        for colour in range(3):
            a, b = times(entry, load(0, 3 * partner + colour), load(1, 3 * partner + colour))
            row.append((
                add_signed(load(0, 3 * s + colour), a),
                add_signed(load(1, 3 * s + colour), b),
            ))
        rows.append(row)
    return rows


def mapped(function, *tables):
    return [
        [
            tuple(function(*[table[s][colour][part] for table in tables]) for part in range(2))
            for colour in range(3)
        ]
        for s in range(2)
    ]


def hop(direction, sign, half_field, link, total):
    for out in range(3):
        row = [link(0, out, inn) for inn in range(3)], [link(1, out, inn) for inn in range(3)]
        moved = []
        for s in range(2):
            re = None
            im = None
            for inn in range(3):
                ure, uim = row[0][inn], row[1][inn]
                hre, him = half_field[s][inn]
                tre = ure * hre - uim * him
                tim = ure * him + uim * hre
                re = tre if re is None else re + tre
                im = tim if im is None else im + tim
            moved.append((re, im))
        for s in range(2):
            for part in range(2):
                total[s][out][part] = add_signed(total[s][out][part], (1.0, moved[s][part]))
        for s in range(2, 4):
            source = 0 if gammas[direction][s][0] != 0 else 1
            entry = gammas[direction][s][source] * sign
            terms = times(entry, *moved[source])
            for part in range(2):
                total[s][out][part] = add_signed(total[s][out][part], terms[part])


def link_loader(links_ref, number, low):
    def link(part, out, inn):
        return links_ref[number, part, out, inn].astype(F32)[low : low + HALF]
    return link


def sideways_kernel(wide_ref, out_ref):
    y = lane_index(HALF) % NY

    def rhs(r, carry):
        for half in range(2):
            low = HALF * half

            def load(part, component):
                return wide_ref[part, r, component, low : low + HALF, :]

            ahead = mapped(
                lambda p: jnp.where(y < NY - 1, turn_lanes(p, -1), turn_lanes(p, NY - 1)),
                projected(3, -1.0, load),
            )
            behind = mapped(
                lambda p: jnp.where(y > 0, turn_lanes(p, 1), turn_lanes(p, 1 - NY)),
                projected(3, 1.0, load),
            )
            for side, field in enumerate((ahead, behind)):
                for s in range(2):
                    for colour in range(3):
                        for part in range(2):
                            out_ref[side, r, 6 * s + 2 * colour + part, low : low + HALF, :] = field[s][colour][part]
        return carry

    lax.fori_loop(0, 4, rhs, 0)


def sideways(wide):
    vm = pl.BlockSpec(memory_space=pltpu.VMEM)
    return pl.pallas_call(
        sideways_kernel,
        out_shape=jax.ShapeDtypeStruct((2, 4, 12, ROWS, LANES), F32),
        in_specs=[vm],
        out_specs=vm,
        compiler_params=vmem_params(8),
        cost_estimate=pl.CostEstimate(flops=40_000_000, bytes_accessed=20_000_000, transcendentals=0),
    )(wide)


def centre_kernel(
    wide_ref, side_ref, when_ref, spin_ref, wall_ref, links_ref, clover_ref, out_ref,
):
    first_time = lax.axis_index("ta") * BLOCK
    upper = row_index(HALF) >= 4

    def rhs(r, carry):
        when = when_ref[r]
        spin = spin_ref[r]
        for half in range(2):
            low = HALF * half

            def load(part, component):
                return wide_ref[part, r, component, low : low + HALF, :]

            total = [[[None, None] for _ in range(3)] for _ in range(4)]
            for side, sign in enumerate((-1.0, 1.0)):
                field = [
                    [
                        tuple(side_ref[side, r, 6 * s + 2 * colour + part, low : low + HALF, :] for part in range(2))
                        for colour in range(3)
                    ]
                    for s in range(2)
                ]
                hop(3, sign, field, link_loader(links_ref, 6 + side, low), total)
            sign = -1.0 if half == 0 else 1.0
            turned = [
                mapped(
                    lambda p: pltpu.roll(p, 4, 0),
                    projected(0, sign, lambda part, c, start=start: wide_ref[part, r, c, start : start + HALF, :]),
                )
                for start in (0, HALF)
            ]
            field = mapped(lambda a, b: jnp.where(upper, b, a), *turned)
            hop(0, sign, field, link_loader(links_ref, half, low), total)
            at_wall = first_time + 2 * half + row_index(HALF) // BLOCK == when
            for chirality in range(2):
                values = [(load(0, 6 * chirality + i), load(1, 6 * chirality + i)) for i in range(6)]
                for i in range(6):
                    re = MASS * values[i][0]
                    im = MASS * values[i][1]
                    for j in range(6):
                        cre = clover_ref[chirality, 0, i, j].astype(F32)[low : low + HALF]
                        cim = clover_ref[chirality, 1, i, j].astype(F32)[low : low + HALF]
                        re = re + (cre * values[j][0] - cim * values[j][1])
                        im = im + (cre * values[j][1] + cim * values[j][0])
                    s = 2 * chirality + i // 3
                    colour = i % 3
                    here = spin == s
                    sre = jnp.where(here, wall_ref[colour, 0, r], 0.0)
                    sim = jnp.where(here, wall_ref[colour, 1, r], 0.0)
                    re = jnp.where(at_wall, sre, 0.0) + (0.5 * total[s][colour][0] - re)
                    im = jnp.where(at_wall, sim, 0.0) + (0.5 * total[s][colour][1] - im)
                    out_ref[r, 6 * chirality + i, low : low + HALF, :] = re
                    out_ref[r, 12 + 6 * chirality + i, low : low + HALF, :] = im
        return carry

    lax.fori_loop(0, 4, rhs, 0)


def centre(wide, side, wall_time, spin_index, wall, links, clover):
    vm = pl.BlockSpec(memory_space=pltpu.VMEM)
    sm = pl.BlockSpec(memory_space=pltpu.SMEM)
    return pl.pallas_call(
        centre_kernel,
        out_shape=jax.ShapeDtypeStruct((4, 24, ROWS, LANES), F32),
        in_specs=[vm] * 2 + [sm] * 3 + [vm] * 2,
        out_specs=vm,
        compiler_params=vmem_params(16),
        cost_estimate=pl.CostEstimate(flops=40_000_000, bytes_accessed=20_000_000, transcendentals=0),
    )(wide, side, wall_time, spin_index, wall, links, clover)


def spread_kernel(stencil_ref, operator_ref):
    def body(k, carry):
        parts = []
        for part in range(2):
            start = pl.multiple_of(48 * k + 24 * part, 24)
            block = stencil_ref[pl.ds(start, 24)].reshape((24 * HALF, 24))
            block = jnp.concatenate([block, jnp.zeros((24 * HALF, LANES - 24), F32)], axis=1)
            block = block + turn_lanes(block, 32)
            parts.append(block + turn_lanes(block, 64))
        operator_ref[k, 0] = parts[0].reshape((24, HALF, LANES))
        operator_ref[k, 1] = parts[1].reshape((24, HALF, LANES))
        operator_ref[k, 2] = (parts[0] + parts[1]).reshape((24, HALF, LANES))
        return carry

    lax.fori_loop(0, 9, body, 0)


def spread(stencil):
    vm = pl.BlockSpec(memory_space=pltpu.VMEM)
    return pl.pallas_call(
        spread_kernel,
        out_shape=jax.ShapeDtypeStruct((9, 3, 24, HALF, LANES), F32),
        in_specs=[vm],
        out_specs=vm,
        compiler_params=vmem_params(8),
    )(stencil)


def fine_kernel(
    wide_ref, partial_ref, xb_ref, tb_ref, zb_ref, ta_ref, za_ref, xa_ref, links_ref, near_ref,
    out_ref, tedge, zedge, xedge, residual, rows_ref,
):
    even = [is_even(axis) for axis in ("ta", "gz", "xy")]
    slabs = ((ta_ref, tb_ref), (za_ref, zb_ref), (xa_ref, xb_ref))
    for direction in range(3):
        for side, sign in enumerate((-1.0, 1.0)):
            toward_a, toward_b = slabs[direction]

            def load(part, component):
                a = toward_a[12 * part + component].astype(F32)
                b = toward_b[12 * part + component].astype(F32)
                return jnp.where(even[direction], a, b) if side == 0 else jnp.where(even[direction], b, a)

            edge = projected(direction, sign, load)
            for s in range(2):
                for colour in range(3):
                    for part in range(2):
                        slot = 6 * s + 2 * colour + part
                        value = edge[s][colour][part]
                        if direction == 0:
                            for r in range(4):
                                tedge[side, slot, r, 0:4, :] = value[4 * r : 4 * r + 4]
                                tedge[side, slot, r, 4:8, :] = value[4 * r : 4 * r + 4]
                        elif direction == 1:
                            zedge[side, slot] = value
                        else:
                            xedge[side, slot] = value
    lanes = lane_index(HALF)
    sub = row_index(HALF)
    upper = sub >= 4
    z = sub % BLOCK

    def rhs(r, carry):
        def table(read):
            return [[tuple(read(6 * s + 2 * colour + part) for part in range(2)) for colour in range(3)] for s in range(2)]

        for half in range(2):
            low = HALF * half

            def loader(start):
                def load(part, component):
                    return wide_ref[part, r, component, start : start + HALF, :]
                return load

            total = [[[None, None] for _ in range(3)] for _ in range(4)]
            side = 1 if half == 0 else 0
            sign = 1.0 if half == 0 else -1.0
            turned = mapped(lambda p: pltpu.roll(p, 4, 0), projected(0, sign, loader(low)))
            edge = table(lambda slot: tedge[side, slot, r])
            lower_part, upper_part = (edge, turned) if half == 0 else (turned, edge)
            field = mapped(lambda a, b: jnp.where(upper, b, a), lower_part, upper_part)
            hop(0, sign, field, link_loader(links_ref, side, low), total)
            for side, sign in enumerate((-1.0, 1.0)):
                row = 4 * r + 2 * half
                first = table(lambda slot: zedge[side, slot, pl.ds(row, 1), :])
                second = table(lambda slot: zedge[side, slot, pl.ds(row + 1, 1), :])
                shift, place = (HALF - 1, 3) if side == 0 else (1, 0)
                field = mapped(
                    lambda p, a, b: jnp.where(z == place, jnp.where(upper, b, a), pltpu.roll(p, shift, 0)),
                    projected(1, sign, loader(low)), first, second,
                )
                hop(1, sign, field, link_loader(links_ref, 2 + side, low), total)
            for side, sign in enumerate((-1.0, 1.0)):
                edge = table(lambda slot: xedge[side, slot, low : low + HALF, :])
                if side == 0:
                    inside = lanes < 96
                    amount = lax.rem(96 - 32 * r + LANES, LANES)
                    shift = LANES - 32
                else:
                    inside = lanes >= 32
                    amount = lax.rem(LANES - 32 * r, LANES)
                    shift = 32
                field = mapped(
                    lambda p, e: jnp.where(inside, pltpu.roll(p, shift, 1), pltpu.roll(e, amount, 1)),
                    projected(2, sign, loader(low)), edge,
                )
                hop(2, sign, field, link_loader(links_ref, 4 + side, low), total)
            for s in range(4):
                for colour in range(3):
                    position = 3 * s + colour
                    re = partial_ref[r, position, low : low + HALF, :] + 0.5 * total[s][colour][0]
                    im = partial_ref[r, 12 + position, low : low + HALF, :] + 0.5 * total[s][colour][1]
                    residual[r, position, low : low + HALF, :] = re
                    residual[r, 12 + position, low : low + HALF, :] = im - re
                    residual[r, 24 + position, low : low + HALF, :] = re + im
        return carry

    lax.fori_loop(0, 4, rhs, 0)

    for part in range(2):
        rows_ref[part] = jnp.zeros((LANES, LANES), F32)

    def vector(v, carry):
        for chirality in range(2):
            acc = [[None] * 3 for _ in range(4)]
            for c in range(6):
                position = 6 * chirality + c
                nre16 = near_ref[v, 0, position].astype(F32)
                nim16 = near_ref[v, 1, position].astype(F32)
                for half in range(2):
                    low = HALF * half
                    nre = nre16[low : low + HALF]
                    nim = nim16[low : low + HALF]
                    factors = (nre - nim, nre, nim)
                    for r in range(4):
                        for form in range(3):
                            term = factors[form] * residual[r, 12 * form + position, low : low + HALF, :]
                            acc[r][form] = term if acc[r][form] is None else acc[r][form] + term
            for r in range(4):
                for part, value in enumerate((acc[r][0] + acc[r][2], acc[r][0] + acc[r][1])):
                    rows_ref[part, pl.ds(r * 32 + chirality * 12 + v, 1), :] = jnp.sum(
                        value, axis=0, keepdims=True
                    )
        return carry

    lax.fori_loop(0, 12, vector, 0, unroll=2)
    member = ((lane_index(HALF) % NY) // BLOCK == row_index(HALF)).astype(F32)
    for part in range(2):
        out_ref[part] = lax.dot_general(
            member, rows_ref[part], (((1,), (1,)), ((), ())),
            precision=lax.Precision.HIGHEST, preferred_element_type=F32,
        )


def fine(wide, partial, halos, links, near):
    vm = pl.BlockSpec(memory_space=pltpu.VMEM)
    return pl.pallas_call(
        fine_kernel,
        out_shape=jax.ShapeDtypeStruct((2, HALF, LANES), F32),
        in_specs=[vm] * 10,
        out_specs=vm,
        scratch_shapes=[
            pltpu.VMEM((2, 12, 4, HALF, LANES), F32),
            pltpu.VMEM((2, 12, ROWS, LANES), F32),
            pltpu.VMEM((2, 12, ROWS, LANES), F32),
            pltpu.VMEM((4, 36, ROWS, LANES), F32),
            pltpu.VMEM((2, LANES, LANES), F32),
        ],
        compiler_params=vmem_params(24),
        cost_estimate=pl.CostEstimate(flops=40_000_000, bytes_accessed=20_000_000, transcendentals=0),
    )(wide, partial, *[halos[i] for i in (5, 1, 3, 0, 2, 4)], links, near)


def merge(low, high, width, inside):
    if high is None:
        high = jnp.zeros_like(low)
    keep = jnp.where(inside, low, high)
    other = jnp.where(inside, high, low)
    return keep + jnp.where(inside, turn_lanes(other, -width), turn_lanes(other, width))


def coarse_step(estimate, neighbours, restricted_ref, operator_ref):
    members = [(re, im - re, re + im) for re, im in [estimate] + neighbours]
    lanes = lane_index(HALF)
    out = []
    sums = [[None] * 24, [None] * 24]
    for i in range(24):
        acc = [None] * 3
        for k in range(9):
            ere, difference, total = members[k]
            terms = (
                operator_ref[k, 2, i] * ere, operator_ref[k, 0, i] * difference, operator_ref[k, 1, i] * total
            )
            for form in range(3):
                acc[form] = terms[form] if acc[form] is None else acc[form] + terms[form]
        sums[0][i] = acc[0] - acc[2]
        sums[1][i] = acc[0] + acc[1]
    for part in range(2):
        values = sums[part] + [None] * 8
        width = 16
        while width >= 1:
            inside = (lanes // width) % 2 == 0
            count = width
            values = [
                None if values[i] is None else merge(values[i], values[i + count], width, inside)
                for i in range(count)
            ]
            width //= 2
        out.append(restricted_ref[part] + values[0])
    return out


def coarse_neighbours(estimate, refs):
    neighbours = []
    for direction, axis in enumerate(("ta", "gz", "xy")):
        even = is_even(axis)
        a = refs[2 * direction]
        b = refs[2 * direction + 1]
        neighbours.append(tuple(jnp.where(even, a[part], b[part]) for part in range(2)))
        neighbours.append(tuple(jnp.where(even, b[part], a[part]) for part in range(2)))
    neighbours.append(tuple(pltpu.roll(value, HALF - 1, 0) for value in estimate))
    neighbours.append(tuple(pltpu.roll(value, 1, 0) for value in estimate))
    return neighbours


def coarse_kernel(e_ref, xa, za, ta, xb, zb, tb, r_ref, operator_ref, out_ref):
    estimate = (e_ref[0], e_ref[1])
    out = coarse_step(estimate, coarse_neighbours(estimate, (ta, tb, za, zb, xa, xb)), r_ref, operator_ref)
    out_ref[0] = out[0]
    out_ref[1] = out[1]


def coarse(estimate, halos, restricted, operator):
    vm = pl.BlockSpec(memory_space=pltpu.VMEM)
    return pl.pallas_call(
        coarse_kernel,
        out_shape=jax.ShapeDtypeStruct((2, HALF, LANES), F32),
        in_specs=[vm] * 9,
        out_specs=vm,
        compiler_params=vmem_params(16),
    )(estimate, *[halos[i] for i in (4, 2, 0, 5, 3, 1)], restricted, operator)


def last_kernel(e_ref, xa, za, ta, xb, zb, tb, r_ref, operator_ref, psi_ref, near_ref, out_hbm, out_ref, wide, sems):
    estimate = (e_ref[0], e_ref[1])
    final = coarse_step(estimate, coarse_neighbours(estimate, (ta, tb, za, zb, xa, xb)), r_ref, operator_ref)
    member = ((lane_index(HALF) % NY) // BLOCK == row_index(HALF)).astype(F32)
    spreads = [
        lax.dot_general(
            final[part], member, (((0,), (0,)), ((), ())),
            precision=lax.Precision.HIGHEST, preferred_element_type=F32,
        )
        for part in range(2)
    ]
    wide[0] = spreads[0]
    wide[1] = spreads[1] - spreads[0]
    wide[2] = spreads[0] + spreads[1]

    def component(c, carry):
        base = (c // 6) * 12
        near = []
        for v in range(12):
            nre = near_ref[v, 0, c].astype(F32)
            nim = near_ref[v, 1, c].astype(F32)
            near.append((nre + nim, nre, nim))
        for r in range(4):
            acc = [None] * 3
            for v in range(12):
                for form in range(3):
                    term = near[v][form] * wide[form, pl.ds(r * 32 + base + v, 1), :]
                    acc[form] = term if acc[form] is None else acc[form] + term
            out_ref[c, 0, r] = psi_ref[0, r, c] + (acc[0] - acc[2])
            out_ref[c, 1, r] = psi_ref[1, r, c] + (acc[0] + acc[1])
        for part in range(2):
            pltpu.make_async_copy(out_ref.at[c, part], out_hbm.at[part, :, c], sems.at[c, part]).start()
        return carry

    lax.fori_loop(0, 12, component, 0, unroll=2)
    for c in range(12):
        for part in range(2):
            pltpu.make_async_copy(out_ref.at[c, part], out_hbm.at[part, :, c], sems.at[c, part]).wait()


def last(estimate, halos, restricted, operator, psi, near):
    vm = pl.BlockSpec(memory_space=pltpu.VMEM)
    return pl.pallas_call(
        last_kernel,
        out_shape=jax.ShapeDtypeStruct((2, 4, 12, ROWS, LANES), F32),
        in_specs=[vm] * 11,
        out_specs=pl.BlockSpec(memory_space=pltpu.HBM),
        scratch_shapes=[
            pltpu.VMEM((12, 2, 4, ROWS, LANES), F32),
            pltpu.VMEM((3, LANES, LANES), F32),
            pltpu.SemaphoreType.DMA((12, 2)),
        ],
        compiler_params=vmem_params(24),
    )(estimate, *[halos[i] for i in (4, 2, 0, 5, 3, 1)], restricted, operator, psi, near)


def exchange(values):
    halos = [None] * 6
    for which in (4, 2, 0, 5, 3, 1):
        halos[which] = swap(values[which], ("ta", "gz", "xy")[which // 2], which % 2)
    return halos


def local(
    fine_solution, links, clover, near_null, coarse_links, wall_time, spin_index, wall_colour
):
    psi = fine_solution.reshape((2, 4, 12, ROWS, LANES))
    links = links.reshape((8, 2, 3, 3, ROWS, LANES))
    clover = clover.reshape((2, 2, 6, 6, ROWS, LANES))
    near = near_null.reshape((12, 2, 12, ROWS, LANES))
    stencil = jnp.transpose(coarse_links, (0, 1, 2, 4, 5, 6, 3)).reshape((9 * 2 * 24, HALF, 24))
    wall = jnp.transpose(wall_colour, (2, 0, 1))
    *slabs, wide = pack(psi)
    halos = exchange(slabs)
    partial = centre(wide, sideways(wide), wall_time, spin_index, wall, links, clover)
    operator = spread(stencil)
    restricted = fine(wide, partial, halos, links, near)
    estimate = restricted
    for step in range(ITERS - 1):
        estimate = coarse(estimate, exchange([estimate] * 6), restricted, operator)
    result = last(estimate, exchange([estimate] * 6), restricted, operator, wide, near)
    return result.reshape(fine_solution.shape)


def solution(mesh):
    placed = (
        P(None, None, None, "ta", "gz", "xy"),
        P(None, None, None, None, "ta", "gz", "xy"),
        P(None, None, None, None, "ta", "gz", "xy"),
        P(None, None, None, "ta", "gz", "xy"),
        P(None, None, None, None, "ta", "gz", "xy"),
        P(),
        P(),
        P(),
    )
    return jax.shard_map(
        local,
        mesh=mesh,
        in_specs=placed,
        out_specs=P(None, None, None, "ta", "gz", "xy"),
        check_vma=False,
    )
```
